32 devices in a mesh: clus: 8 (over z, x), sub: 4 (over y, core).
Axes of the slice: x: 2, y: 2, z: 4, core: 2. Of those that a mesh axis runs over, the one named last changes fastest.
Arguments:
- forward_rhs: bfloat16 [256, 32, 256], P('clus', 'sub'), may hold values from -6 to 6
- adjoint_rhs: bfloat16 [256, 32, 256], P('clus', 'sub'), may hold values from -6 to 6
- far_clusters: int32 [2, 4096], P(None, ('clus', 'sub')), may hold values from 0 to 255, as said below
- far_ranks: int32 [4096], P(('clus', 'sub')), may hold values from 0 to 32, as said below
- far_left: bfloat16 [4096, 2, 32, 128], P(('clus', 'sub')), may hold values from -0.25 to 0.25
- far_right: bfloat16 [4096, 2, 32, 128], P(('clus', 'sub')), may hold values from -0.5 to 0.5
- near_clusters: int32 [2, 1024], P(None, ('clus', 'sub')), may hold values from 0 to 255, as said below
- near_blocks: bfloat16 [1024, 2, 128, 128], P(('clus', 'sub')), may hold values from -0.125 to 0.125
- panel_params: int32 [4, 32768], P(None, 'clus'), may hold values from 0 to 4095, as said below
- panel_weights: float32 [4, 32768], P(None, 'clus'), may hold values from -6 to 6
- panel_counts: int32 [32768], P('clus'), may hold values from 1 to 4
Outputs:
- forward_field: float32 [256, 32, 256], P('clus', 'sub')
- adjoint_field: float32 [256, 32, 256], P('clus', 'sub')
- param_gradient: float32 [4096], P(('clus', 'sub'))
The draws below stay inside these ranges and needn't reach their ends.
Inputs may be any that keep to these rules, and one draw needn't show every extreme that they name: `far_clusters`: block slot b belongs to device b // 128; its row cluster lies in row group g = (b // 128) // 4, among clusters 32 * g to 32 * g + 31; its column cluster is the row cluster plus d modulo 256 with 2 <= |d| <= 32. `far_ranks`: 0 marks an empty slot; on each device the live slots come first. `near_clusters`: block slot b belongs to device b // 32; its row cluster lies in row group (b // 32) // 4; its column cluster is the row cluster plus d modulo 256 with |d| <= 1. panel_params[0,p] equals p // 8 plus an offset of -3 to 3, modulo 4096; the other slots may name any shape parameter.
All inputs are finite; a program needn't handle non-finite values.
Results may differ from the reference program's by a relative error of at most 0.0036.
Values may be sent and summed in bfloat16 or wider, within the bound.
No kernel may reach another device: no remote copies, remote signals or barrier semaphores. Data moves between devices by JAX's collectives and lax.ppermute only.
A program may use at most 128 MiB of HBM per device.

```python
import jax
import jax.numpy as jnp
from jax import lax

CS = 128
RANK = 32
NRHS = 32
PSLOT = 4
CG = 32
FAR_DEV = 128
NEAR_DEV = 32
MEMBERS = 4
NC = 256
NP = 32768
NPAR = 4096
PPP = 8
FAR_ALL = 4096
NEAR_ALL = 1024


def draw_far_clusters(key, part):
    key_rows, key_magnitude, key_signs = jax.random.split(jax.random.fold_in(key, 11), 3)
    slot_total = FAR_ALL
    flat_index = jnp.arange(slot_total, dtype=jnp.int32)
    group_ids = flat_index // FAR_DEV // MEMBERS
    within_group = jax.random.randint(key_rows, (slot_total,), 0, CG, dtype=jnp.int32)
    within_group = within_group.at[0].set(0).at[slot_total - 1].set(CG - 1)
    row_ids = group_ids * CG + within_group
    offsets = jax.random.randint(key_magnitude, (slot_total,), 2, CG + 1, dtype=jnp.int32)
    signs = jax.random.randint(key_signs, (slot_total,), 0, 2, dtype=jnp.int32) * 2 - 1
    col_ids = (row_ids + offsets * signs) % NC
    return jnp.stack([row_ids, col_ids]).astype(jnp.int32)


def draw_far_ranks(key, part):
    key_live, key_ranks = jax.random.split(jax.random.fold_in(key, 23), 2)
    device_total = FAR_ALL // FAR_DEV
    flat_index = jnp.arange(FAR_ALL, dtype=jnp.int32)
    device_ids = flat_index // FAR_DEV
    slot_ids = flat_index % FAR_DEV
    live_counts = jax.random.randint(key_live, (device_total,), FAR_DEV // 2, FAR_DEV + 1, dtype=jnp.int32)
    live_counts = live_counts.at[0].set(FAR_DEV).at[device_total - 1].set(FAR_DEV // 2)
    rank_draw = jax.random.randint(key_ranks, (FAR_ALL,), 1, RANK + 1, dtype=jnp.int32)
    rank_draw = rank_draw.at[0].set(RANK)
    return jnp.where(slot_ids < live_counts[device_ids], rank_draw, 0).astype(jnp.int32)


def draw_near_clusters(key, part):
    key_rows, key_offsets = jax.random.split(jax.random.fold_in(key, 37), 2)
    slot_total = NEAR_ALL
    flat_index = jnp.arange(slot_total, dtype=jnp.int32)
    group_ids = flat_index // NEAR_DEV // MEMBERS
    within_group = jax.random.randint(key_rows, (slot_total,), 0, CG, dtype=jnp.int32)
    within_group = within_group.at[0].set(0).at[slot_total - 1].set(CG - 1)
    row_ids = group_ids * CG + within_group
    offsets = jax.random.randint(key_offsets, (slot_total,), -1, 2, dtype=jnp.int32)
    offsets = offsets.at[0].set(0).at[slot_total - 1].set(0)
    col_ids = (row_ids + offsets) % NC
    return jnp.stack([row_ids, col_ids]).astype(jnp.int32)


def draw_panel_params(key, part):
    key_offsets, key_global = jax.random.split(jax.random.fold_in(key, 41), 2)
    home_params = jnp.arange(NP, dtype=jnp.int32) // PPP
    offsets = jax.random.randint(key_offsets, (NP,), -3, 4, dtype=jnp.int32)
    local_slot = (home_params + offsets) % NPAR
    global_slots = jax.random.randint(key_global, (PSLOT - 1, NP), 0, NPAR, dtype=jnp.int32)
    global_slots = global_slots.at[0, 0].set(NPAR - 1).at[0, 1].set(0)
    return jnp.concatenate([local_slot[None, :], global_slots], axis=0).astype(jnp.int32)


def draw_panel_counts(key, part):
    key_counts = jax.random.fold_in(key, 53)
    counts = jax.random.randint(key_counts, (NP,), 1, PSLOT + 1, dtype=jnp.int32)
    return counts.at[0].set(PSLOT).at[1].set(PSLOT).at[2].set(1).astype(jnp.int32)


def level_of(own_key, dims, pieces, smallest, top_value):
    gain = 1.0
    for axis_at, shards_of in pieces:
        draws = jax.random.uniform(jax.random.fold_in(jax.random.fold_in(own_key, 6), axis_at), (shards_of,), jnp.float32, smallest / len(pieces), top_value / len(pieces))
        gain = gain * jnp.repeat(jnp.exp(draws), dims[axis_at] // shards_of).reshape((-1,) + (1,) * (len(dims) - 1 - axis_at))
    return gain


def gaussian(stream_key, dims, spread, most, shards=(), held_as=jnp.bfloat16):
    entries = jax.random.normal(stream_key, dims, jnp.float32) * spread
    if len(shards) > 0:
        entries = level_of(stream_key, dims, shards, -0.22, 0.18) * entries
    return jnp.clip(entries, min=-most, max=most).astype(held_as)


def setup_inputs(seed: int = 0) -> dict:
    keys = jax.random.split(jax.random.key(seed), 12)
    forward_rhs = gaussian(keys[0], (NC, NRHS, 2 * CS), 1.0, 6.0, ((0, 8), (1, 4)))
    adjoint_rhs = gaussian(keys[1], (NC, NRHS, 2 * CS), 1.0, 6.0, ((0, 8), (1, 4)))
    far_clusters = draw_far_clusters(jax.random.fold_in(keys[11], 71), 0)
    far_ranks = draw_far_ranks(jax.random.fold_in(keys[11], 71), 0)
    far_left = gaussian(keys[4], (FAR_ALL, 2, RANK, CS), (16 * RANK) ** -0.5, 0.25, ((0, 32),))
    far_right = gaussian(keys[5], (FAR_ALL, 2, RANK, CS), CS ** -0.5, 0.5, ((0, 32),))
    near_clusters = draw_near_clusters(jax.random.fold_in(keys[11], 71), 0)
    near_blocks = gaussian(keys[7], (NEAR_ALL, 2, CS, CS), (16 * CS) ** -0.5, 0.125, ((0, 32),))
    panel_params = draw_panel_params(jax.random.fold_in(keys[11], 71), 0)
    panel_weights = gaussian(keys[9], (PSLOT, NP), 1.0, 6.0, ((1, 8),), jnp.float32)
    panel_counts = draw_panel_counts(jax.random.fold_in(keys[11], 71), 0)
    return {"forward_rhs": forward_rhs, "adjoint_rhs": adjoint_rhs, "far_clusters": far_clusters, "far_ranks": far_ranks, "far_left": far_left, "far_right": far_right, "near_clusters": near_clusters, "near_blocks": near_blocks, "panel_params": panel_params, "panel_weights": panel_weights, "panel_counts": panel_counts}


def complex_mix(lhs_data, rhs_factor, einsum_form):
    width = lhs_data.shape[-1] // 2
    real_lhs = lhs_data[..., :width].astype(jnp.float32)
    imag_lhs = lhs_data[..., width:].astype(jnp.float32)
    real_rhs = rhs_factor[:, 0].astype(jnp.float32)
    imag_rhs = rhs_factor[:, 1].astype(jnp.float32)
    real_out = jnp.einsum(einsum_form, real_lhs, real_rhs) - jnp.einsum(einsum_form, imag_lhs, imag_rhs)
    imag_out = jnp.einsum(einsum_form, real_lhs, imag_rhs) + jnp.einsum(einsum_form, imag_lhs, real_rhs)
    return jnp.concatenate([real_out, imag_out], axis=-1)


def rank_columns(rank_list, width):
    column_ids = lax.broadcasted_iota(jnp.int32, (rank_list.shape[0], width), 1)
    kept = (column_ids < rank_list[:, None]).astype(jnp.float32)
    return jnp.concatenate([kept, kept], axis=1)[:, None, :]


def reference(forward_rhs, adjoint_rhs, far_clusters, far_ranks, far_left, far_right, near_clusters, near_blocks, panel_params, panel_weights, panel_counts):
    cluster_total = forward_rhs.shape[0]
    far_groups = far_ranks.shape[0] // FAR_DEV
    near_groups = near_blocks.shape[0] // NEAR_DEV
    far_pairs = far_clusters.reshape(2, far_groups, FAR_DEV).transpose(1, 0, 2)
    near_pairs = near_clusters.reshape(2, near_groups, NEAR_DEV).transpose(1, 0, 2)

    def far_step(state_pair, batch):
        fwd_acc, adj_acc = state_pair
        pair_ids, rank_list, left_factor, right_factor = batch
        row_ids = pair_ids[0]
        col_ids = pair_ids[1]
        kept = rank_columns(rank_list, left_factor.shape[2])
        coeff = (complex_mix(forward_rhs[col_ids], right_factor, "bkq,bjq->bkj") * kept).astype(jnp.bfloat16)
        coeff = lax.optimization_barrier(coeff)
        fwd_acc = fwd_acc + jax.ops.segment_sum(complex_mix(coeff, left_factor, "bkj,bjp->bkp"), row_ids, num_segments=cluster_total)
        back_coeff = (complex_mix(adjoint_rhs[row_ids], left_factor, "bkp,bjp->bkj") * kept).astype(jnp.bfloat16)
        back_coeff = lax.optimization_barrier(back_coeff)
        adj_acc = adj_acc + jax.ops.segment_sum(complex_mix(back_coeff, right_factor, "bkj,bjq->bkq"), col_ids, num_segments=cluster_total)
        return (fwd_acc, adj_acc), None

    def near_step(state_pair, batch):
        fwd_acc, adj_acc = state_pair
        pair_ids, dense_block = batch
        row_ids = pair_ids[0]
        col_ids = pair_ids[1]
        fwd_acc = fwd_acc + jax.ops.segment_sum(complex_mix(forward_rhs[col_ids], dense_block, "bkq,bpq->bkp"), row_ids, num_segments=cluster_total)
        adj_acc = adj_acc + jax.ops.segment_sum(complex_mix(adjoint_rhs[row_ids], dense_block, "bkp,bpq->bkq"), col_ids, num_segments=cluster_total)
        return (fwd_acc, adj_acc), None

    zero_field = jnp.zeros(forward_rhs.shape, jnp.float32)
    far_batches = (far_pairs, far_ranks.reshape(far_groups, FAR_DEV),
                   far_left.reshape((far_groups, FAR_DEV) + far_left.shape[1:]),
                   far_right.reshape((far_groups, FAR_DEV) + far_right.shape[1:]))
    state_pair, _ = lax.scan(far_step, (zero_field, zero_field), far_batches)
    near_batches = (near_pairs, near_blocks.reshape((near_groups, NEAR_DEV) + near_blocks.shape[1:]))
    state_pair, _ = lax.scan(near_step, state_pair, near_batches)
    forward_field, adjoint_field = state_pair
    half_width = forward_field.shape[-1] // 2
    sensitivity = jnp.sum(forward_field[..., :half_width] * adjoint_field[..., :half_width]
                          - forward_field[..., half_width:] * adjoint_field[..., half_width:], axis=1).reshape(-1) / forward_rhs.shape[1]
    slot_ids = lax.broadcasted_iota(jnp.int32, panel_params.shape, 0)
    live_slots = slot_ids < panel_counts[None, :]
    weighted = jnp.where(live_slots, panel_weights * sensitivity[None, :], jnp.zeros(panel_weights.shape, panel_weights.dtype))
    param_gradient = jax.ops.segment_sum(weighted.reshape(-1), panel_params.reshape(-1), num_segments=NPAR)
    return forward_field, adjoint_field, param_gradient
```

```python
import functools

import jax
import jax.numpy as jnp
from jax import lax
from jax.experimental import pallas as pl
from jax.experimental.pallas import tpu as pltpu
from jax.sharding import PartitionSpec as P

PAR_DEV = 128
AXES = ("clus", "sub")
FAR_UNROLL = 16
NEAR_UNROLL = 4
VMEM_BYTES = 40 * 1024 * 1024


def moved(x, by, mask):
    groups, members = lax.axis_size("clus"), lax.axis_size("sub")
    pairs = [
        (g * members + s, ((g + by) % groups) * members + (s ^ mask))
        for g in range(groups)
        for s in range(members)
    ]
    return lax.ppermute(x, AXES, pairs)


def wide_place(cluster, row, clusters, total):
    first = row - lax.rem(row, clusters)
    place = lax.rem(cluster - first + total, total)
    return jnp.where(place >= 2 * clusters, place - (total - 3 * clusters), place)


def block_kernel(transposed, total, members, *refs):
    far_ids, ranks, near_ids = refs[:3]
    halves = 1 if transposed else 3
    pieces = refs[3 : 3 + halves * members]
    first, second, near = refs[3 + halves * members : 6 + halves * members]
    outs = refs[6 + halves * members : 6 + halves * members + members]
    lhs, coeffs = refs[6 + halves * members + members :]
    clusters, height, _ = pieces[0].shape
    far, _, rank, width = first.shape
    near_total = near.shape[0]
    rows = lhs.shape[1]
    part = 2 * height
    for out in outs:
        out[...] = jnp.zeros_like(out)
    for g in range(halves):

        @pl.loop(0, clusters, unroll=2)
        def _(c):
            left, right = [], []
            for piece in pieces[g * members : (g + 1) * members]:
                x = piece[c].astype(jnp.float32)
                re, im = x[:, :width], x[:, width:]
                left += [re, im]
                right += [-im, re]
            both = [jnp.concatenate(left, axis=0), jnp.concatenate(right, axis=0)]
            lhs[g * clusters + c] = jnp.concatenate(both, axis=1).astype(jnp.bfloat16)

    def add(place, value):
        for i, out in enumerate(outs):
            out[place] += value[i * part : (i + 1) * part]

    def places(ids, b):
        row = ids[0, b]
        column = wide_place(ids[1, b], row, clusters, total)
        row = lax.rem(row, clusters)
        return (row, column) if transposed else (column, row)

    rank_ids = lax.broadcasted_iota(jnp.int32, (rows, 2 * rank), 1)
    rank_ids = jnp.where(rank_ids >= rank, rank_ids - rank, rank_ids)

    far_unroll = min(FAR_UNROLL, far)
    near_unroll = min(NEAR_UNROLL, near_total)

    @pl.loop(0, far // far_unroll)
    def _(t):
        for i in range(far_unroll):
            b = t * far_unroll + i
            re, im = first[b, 0], first[b, 1]
            factor = jnp.concatenate(
                [jnp.concatenate([re, im], axis=1), jnp.concatenate([-im, re], axis=1)], axis=0
            )
            coeff = lax.dot_general(
                lhs[places(far_ids, b)[0]],
                factor,
                (((1,), (1,)), ((), ())),
                preferred_element_type=jnp.float32,
            )
            coeffs[i] = jnp.where(rank_ids < ranks[b], coeff, 0.0).astype(jnp.bfloat16)
        for i in range(far_unroll):
            b = t * far_unroll + i
            value = jnp.dot(
                coeffs[i], second[b].reshape(2 * rank, width), preferred_element_type=jnp.float32
            )
            add(places(far_ids, b)[1], value)

    @pl.loop(0, near_total // near_unroll)
    def _(t):
        for i in range(near_unroll):
            b = t * near_unroll + i
            source, place = places(near_ids, b)
            if transposed:
                value = jnp.dot(
                    lhs[source],
                    near[b].reshape(2 * width, width),
                    preferred_element_type=jnp.float32,
                )
            else:
                value = lax.dot_general(
                    lhs[source],
                    jnp.concatenate([near[b, 0], near[b, 1]], axis=1),
                    (((1,), (1,)), ((), ())),
                    preferred_element_type=jnp.float32,
                )
            add(place, value)


def apply_blocks(transposed, total, members, far_ids, ranks, near_ids, pieces, first, second, near):
    clusters, height, double = pieces[0].shape
    halves = len(pieces) // members
    out_clusters = 3 * clusters if transposed else clusters
    rows = members * 2 * height
    rank, width = first.shape[2:]
    smem = pl.BlockSpec(memory_space=pltpu.SMEM)
    vmem = pl.BlockSpec(memory_space=pltpu.VMEM)
    flops = 2 * rows * (first.shape[0] * 2 * 2 * rank * 2 * width + near.shape[0] * 2 * width * width)
    return pl.pallas_call(
        functools.partial(block_kernel, transposed, total, members),
        in_specs=[smem] * 3 + [vmem] * (len(pieces) + 3),
        out_specs=[vmem] * members,
        out_shape=[
            jax.ShapeDtypeStruct((out_clusters, 2 * height, width), jnp.float32)
        ] * members,
        scratch_shapes=[
            pltpu.VMEM((halves * clusters, rows, double), jnp.bfloat16),
            pltpu.VMEM((min(FAR_UNROLL, first.shape[0]), rows, 2 * rank), jnp.bfloat16),
        ],
        compiler_params=pltpu.CompilerParams(vmem_limit_bytes=VMEM_BYTES),
        cost_estimate=pl.CostEstimate(flops=flops, bytes_accessed=20_000_000, transcendentals=0),
    )(far_ids, ranks, near_ids, *pieces, first, second, near)


def final_kernel(column_total, n_fwd, n_adj, *refs):
    fwd_terms = refs[:n_fwd]
    adj_terms = refs[n_fwd : n_fwd + n_adj]
    params, weights, counts = refs[n_fwd + n_adj : n_fwd + n_adj + 3]
    fwd_out, adj_out, grad = refs[n_fwd + n_adj + 3 :]
    clusters, height, _ = fwd_out.shape
    slots = params.shape[0]
    high, width = grad.shape
    high_ids = lax.broadcasted_iota(jnp.int32, (high, width), 0)
    low_ids = lax.broadcasted_iota(jnp.int32, (width, width), 0)
    shift = width.bit_length() - 1
    grad[...] = jnp.zeros_like(grad)

    def panels(c):
        fwd = sum(t[c].astype(jnp.float32) for t in fwd_terms)
        adj = sum(t[c].astype(jnp.float32) for t in adj_terms)
        for out, value in ((fwd_out, fwd), (adj_out, adj)):
            out[c, :, :width] = value[:height]
            out[c, :, width:] = value[height:]
        product = fwd * adj
        sens = jnp.sum(product[:height] - product[height:], axis=0, keepdims=True) / column_total
        at = pl.ds(pl.multiple_of(c * width, width), width)
        slot_ids = lax.broadcasted_iota(jnp.int32, (slots, width), 0)
        value = jnp.where(slot_ids < counts[:, at], weights[:, at] * sens, 0.0)
        ids = params[:, at]
        high_of, low_of = ids >> shift, ids & (width - 1)
        top = value.astype(jnp.bfloat16).astype(jnp.float32)
        rest = value - top
        middle = rest.astype(jnp.bfloat16).astype(jnp.float32)
        terms = (top, middle, rest - middle)
        spread, places = [], []
        for m in range(slots):
            row = slice(m, m + 1)
            hit = high_ids == high_of[row]
            spread.append(
                jnp.concatenate([jnp.where(hit, t[row], 0.0) for t in terms], axis=0).astype(jnp.bfloat16)
            )
            places.append(jnp.where(low_ids == low_of[row], 1.0, 0.0).astype(jnp.bfloat16))
        got = lax.dot_general(
            jnp.concatenate(spread, axis=1),
            jnp.concatenate(places, axis=1),
            (((1,), (1,)), ((), ())),
            preferred_element_type=jnp.float32,
        )
        grad[...] += sum(got[k * high : (k + 1) * high] for k in range(len(terms)))

    @pl.loop(0, clusters, unroll=4)
    def _(c):
        panels(c)


def finish(column_total, fwd_terms, adj_terms, params, weights, counts, high):
    clusters, part, width = fwd_terms[0].shape
    vmem = pl.BlockSpec(memory_space=pltpu.VMEM)
    first_clusters = pl.BlockSpec((clusters, part, width), lambda i: (0, 0, 0))
    field = jax.ShapeDtypeStruct((clusters, part // 2, 2 * width), jnp.float32)
    whole = lambda shape: pl.BlockSpec(shape, lambda i: (0,) * len(shape))
    terms = [*fwd_terms, *adj_terms]
    return pl.pallas_call(
        functools.partial(final_kernel, column_total, len(fwd_terms), len(adj_terms)),
        grid=(1,),
        in_specs=[first_clusters] * len(terms)
        + [whole(params.shape), whole(weights.shape), whole(counts.shape)],
        out_specs=[whole(field.shape), whole(field.shape), whole((high, width))],
        out_shape=[field, field, jax.ShapeDtypeStruct((high, width), jnp.float32)],
        compiler_params=pltpu.CompilerParams(vmem_limit_bytes=VMEM_BYTES),
        cost_estimate=pl.CostEstimate(flops=200_000_000, bytes_accessed=3_000_000, transcendentals=0),
    )(*terms, params, weights, counts)


def shards(
    forward_rhs,
    adjoint_rhs,
    far_clusters,
    far_ranks,
    far_left,
    far_right,
    near_clusters,
    near_blocks,
    panel_params,
    panel_weights,
    panel_counts,
):
    groups = lax.axis_size("clus")
    members = lax.axis_size("sub")
    clusters = forward_rhs.shape[0]
    total = clusters * groups
    column_total = forward_rhs.shape[1] * members
    evens = range(0, members, 2)

    def all_columns(mine):
        pieces = []
        for x in mine:
            pieces += [x, moved(x, 0, 1)]
        return pieces

    w_mine = [adjoint_rhs if m == 0 else moved(adjoint_rhs, 0, m) for m in evens]
    w_pieces = all_columns(w_mine)
    x_next, x_prev = moved(forward_rhs, -1, 0), moved(forward_rhs, 1, 0)
    x_pieces = []
    for x in (forward_rhs, x_next, x_prev):
        x_pieces += all_columns([x if m == 0 else moved(x, 0, m) for m in evens])

    apply = functools.partial(apply_blocks, total=total, members=members)
    adj_parts = apply(
        True, far_ids=far_clusters, ranks=far_ranks, near_ids=near_clusters,
        pieces=w_pieces, first=far_left, second=far_right, near=near_blocks,
    )
    adj_core = [moved(adj_parts[m + 1], 0, 1) for m in evens]
    fwd_parts = apply(
        False, far_ids=far_clusters, ranks=far_ranks, near_ids=near_clusters,
        pieces=x_pieces, first=far_right, second=far_left, near=near_blocks,
    )
    fwd_core = [moved(fwd_parts[m + 1], 0, 1) for m in evens]

    sides, own = [], []
    for k, m in enumerate(evens):
        if m:
            both = adj_parts[m] + adj_core[k]
            sides.append(moved(both[clusters:].astype(jnp.bfloat16), 0, m))
            own.append(moved(both[:clusters].astype(jnp.bfloat16), 0, m))
    side = adj_parts[0][clusters:] + adj_core[0][clusters:]
    for s in sides:
        side = side + s.astype(jnp.float32)
    side = side.astype(jnp.bfloat16)
    ring = [moved(side[:clusters], 1, 0), moved(side[clusters:], -1, 0)]
    adj_terms = [adj_parts[0], adj_core[0], *own, *ring]

    fwd_terms = [fwd_parts[0], fwd_core[0]]
    for k, m in enumerate(evens):
        if m:
            fwd_terms.append(moved((fwd_parts[m] + fwd_core[k]).astype(jnp.bfloat16), 0, m))

    devices = groups * members
    forward_field, adjoint_field, spread = finish(
        column_total, fwd_terms, adj_terms, panel_params, panel_weights, panel_counts[None, :],
        PAR_DEV * devices // near_blocks.shape[-1],
    )
    pieces = lax.all_to_all(spread.reshape(devices, PAR_DEV), AXES, 0, 0, tiled=True)
    return forward_field, adjoint_field, jnp.sum(pieces, axis=0)


def solution(mesh):
    in_specs = (
        P("clus", "sub", None),
        P("clus", "sub", None),
        P(None, ("clus", "sub")),
        P(("clus", "sub")),
        P(("clus", "sub"), None, None, None),
        P(("clus", "sub"), None, None, None),
        P(None, ("clus", "sub")),
        P(("clus", "sub"), None, None, None),
        P(None, "clus"),
        P(None, "clus"),
        P("clus"),
    )
    out_specs = (P("clus", "sub", None), P("clus", "sub", None), P(("clus", "sub")))
    return jax.shard_map(shards, mesh=mesh, in_specs=in_specs, out_specs=out_specs, check_vma=False)
```

```python
import functools

import jax
import jax.numpy as jnp
from jax import lax
from jax.experimental import pallas as pl
from jax.experimental.pallas import tpu as pltpu
from jax.sharding import PartitionSpec as P

PAR_DEV = 128
AXES = ("clus", "sub")
FAR_UNROLL = 16
NEAR_UNROLL = 4
VMEM_BYTES = 40 * 1024 * 1024
LOAD_BYTES = 40 * 1024 * 1024


def moved(x, by, mask):
    groups, members = lax.axis_size("clus"), lax.axis_size("sub")
    pairs = [
        (g * members + s, ((g + by) % groups) * members + (s ^ mask))
        for g in range(groups)
        for s in range(members)
    ]
    return lax.ppermute(x, AXES, pairs)


def wide_place(cluster, row, clusters, total):
    first = row - lax.rem(row, clusters)
    place = lax.rem(cluster - first + total, total)
    return jnp.where(place >= 2 * clusters, place - (total - 3 * clusters), place)


def block_kernel(transposed, total, members, *refs):
    tables_in = refs[:3]
    halves = 1 if transposed else 3
    pieces = refs[3 : 3 + halves * members]
    first, second, near = refs[3 + halves * members : 6 + halves * members]
    outs = refs[6 + halves * members : 6 + halves * members + members]
    lhs, coeffs, far_ids, ranks, near_ids, sems = refs[6 + halves * members + members :]
    tables = (far_ids, ranks, near_ids)
    copies = [pltpu.make_async_copy(a, b, sems.at[i]) for i, (a, b) in enumerate(zip(tables_in, tables))]
    for copy in copies:
        copy.start()
    clusters, height, _ = pieces[0].shape
    far, _, rank, width = first.shape
    near_total = near.shape[0]
    rows = lhs.shape[1]
    part = 2 * height
    for out in outs:
        out[...] = jnp.zeros_like(out)
    for g in range(halves):

        @pl.loop(0, clusters, unroll=2)
        def _(c):
            left, right = [], []
            for piece in pieces[g * members : (g + 1) * members]:
                x = piece[c].astype(jnp.float32)
                re, im = x[:, :width], x[:, width:]
                left += [re, im]
                right += [-im, re]
            both = [jnp.concatenate(left, axis=0), jnp.concatenate(right, axis=0)]
            lhs[g * clusters + c] = jnp.concatenate(both, axis=1).astype(jnp.bfloat16)

    for copy in copies:
        copy.wait()

    def add(place, value):
        for i, out in enumerate(outs):
            out[place] += value[i * part : (i + 1) * part]

    def places(ids, b):
        row = ids[0, b]
        column = wide_place(ids[1, b], row, clusters, total)
        row = lax.rem(row, clusters)
        return (row, column) if transposed else (column, row)

    rank_ids = lax.broadcasted_iota(jnp.int32, (rows, 2 * rank), 1)
    rank_ids = jnp.where(rank_ids >= rank, rank_ids - rank, rank_ids)

    far_unroll = min(FAR_UNROLL, far)
    near_unroll = min(NEAR_UNROLL, near_total)

    @pl.loop(0, far // far_unroll)
    def _(t):
        for i in range(far_unroll):
            b = t * far_unroll + i
            re, im = first[b, 0], first[b, 1]
            factor = jnp.concatenate(
                [jnp.concatenate([re, im], axis=1), jnp.concatenate([-im, re], axis=1)], axis=0
            )
            coeff = lax.dot_general(
                lhs[places(far_ids, b)[0]],
                factor,
                (((1,), (1,)), ((), ())),
                preferred_element_type=jnp.float32,
            )
            coeffs[i] = jnp.where(rank_ids < ranks[b], coeff, 0.0).astype(jnp.bfloat16)
        for i in range(far_unroll):
            b = t * far_unroll + i
            value = jnp.dot(
                coeffs[i], second[b].reshape(2 * rank, width), preferred_element_type=jnp.float32
            )
            add(places(far_ids, b)[1], value)

    @pl.loop(0, near_total // near_unroll)
    def _(t):
        for i in range(near_unroll):
            b = t * near_unroll + i
            source, place = places(near_ids, b)
            if transposed:
                value = jnp.dot(
                    lhs[source],
                    near[b].reshape(2 * width, width),
                    preferred_element_type=jnp.float32,
                )
            else:
                value = lax.dot_general(
                    lhs[source],
                    jnp.concatenate([near[b, 0], near[b, 1]], axis=1),
                    (((1,), (1,)), ((), ())),
                    preferred_element_type=jnp.float32,
                )
            add(place, value)


def apply_blocks(transposed, total, members, far_ids, ranks, near_ids, pieces, first, second, near):
    clusters, height, double = pieces[0].shape
    halves = len(pieces) // members
    out_clusters = 3 * clusters if transposed else clusters
    rows = members * 2 * height
    rank, width = first.shape[2:]
    anywhere = pl.BlockSpec(memory_space=pl.ANY)
    vmem = pl.BlockSpec(memory_space=pltpu.VMEM)
    tables = (far_ids, ranks, near_ids)
    flops = 2 * rows * (first.shape[0] * 2 * 2 * rank * 2 * width + near.shape[0] * 2 * width * width)
    return pl.pallas_call(
        functools.partial(block_kernel, transposed, total, members),
        in_specs=[anywhere] * 3 + [vmem] * (len(pieces) + 3),
        out_specs=[vmem] * members,
        out_shape=[
            jax.ShapeDtypeStruct((out_clusters, 2 * height, width), jnp.float32)
        ] * members,
        scratch_shapes=[
            pltpu.VMEM((halves * clusters, rows, double), jnp.bfloat16),
            pltpu.VMEM((min(FAR_UNROLL, first.shape[0]), rows, 2 * rank), jnp.bfloat16),
            *[pltpu.SMEM(t.shape, t.dtype) for t in tables],
            pltpu.SemaphoreType.DMA((len(tables),)),
        ],
        compiler_params=pltpu.CompilerParams(vmem_limit_bytes=VMEM_BYTES),
        cost_estimate=pl.CostEstimate(flops=flops, bytes_accessed=20_000_000, transcendentals=0),
    )(*tables, *pieces, first, second, near)


def load_kernel(parts, *refs):
    count = (len(refs) - 1) // 2
    sources, targets, sems = refs[:count], refs[count : 2 * count], refs[2 * count]
    copies = []
    for i, (source, target) in enumerate(zip(sources, targets)):
        length = source.shape[0] // parts
        for k in range(parts):
            at = pl.ds(k * length, length)
            copies.append(pltpu.make_async_copy(source.at[at], target.at[at], sems.at[i, k]))
    for copy in copies:
        copy.start()
    for copy in copies:
        copy.wait()


def loaded(*arrays):
    parts = 4
    return pl.pallas_call(
        functools.partial(load_kernel, parts),
        in_specs=[pl.BlockSpec(memory_space=pltpu.HBM)] * len(arrays),
        out_specs=[pl.BlockSpec(memory_space=pltpu.VMEM)] * len(arrays),
        out_shape=[jax.ShapeDtypeStruct(a.shape, a.dtype) for a in arrays],
        scratch_shapes=[pltpu.SemaphoreType.DMA((len(arrays), parts))],
        compiler_params=pltpu.CompilerParams(vmem_limit_bytes=LOAD_BYTES),
        cost_estimate=pl.CostEstimate(flops=0, bytes_accessed=12_000_000, transcendentals=0),
    )(*arrays)


def final_kernel(column_total, n_fwd, n_adj, *refs):
    fwd_terms = refs[:n_fwd]
    adj_terms = refs[n_fwd : n_fwd + n_adj]
    params, weights, counts = refs[n_fwd + n_adj : n_fwd + n_adj + 3]
    fwd_out, adj_out, grad = refs[n_fwd + n_adj + 3 :]
    clusters, height, _ = fwd_out.shape
    slots = params.shape[0]
    high, width = grad.shape
    high_ids = lax.broadcasted_iota(jnp.int32, (high, width), 0)
    low_ids = lax.broadcasted_iota(jnp.int32, (width, width), 0)
    shift = width.bit_length() - 1
    grad[...] = jnp.zeros_like(grad)

    def panels(c):
        fwd = sum(t[c].astype(jnp.float32) for t in fwd_terms)
        adj = sum(t[c].astype(jnp.float32) for t in adj_terms)
        for out, value in ((fwd_out, fwd), (adj_out, adj)):
            out[c, :, :width] = value[:height]
            out[c, :, width:] = value[height:]
        product = fwd * adj
        sens = jnp.sum(product[:height] - product[height:], axis=0, keepdims=True) / column_total
        at = pl.ds(pl.multiple_of(c * width, width), width)
        slot_ids = lax.broadcasted_iota(jnp.int32, (slots, width), 0)
        value = jnp.where(slot_ids < counts[:, at], weights[:, at] * sens, 0.0)
        ids = params[:, at]
        high_of, low_of = ids >> shift, ids & (width - 1)
        top = value.astype(jnp.bfloat16).astype(jnp.float32)
        rest = value - top
        middle = rest.astype(jnp.bfloat16).astype(jnp.float32)
        terms = (top, middle, rest - middle)
        spread, places = [], []
        for m in range(slots):
            row = slice(m, m + 1)
            hit = high_ids == high_of[row]
            spread.append(
                jnp.concatenate([jnp.where(hit, t[row], 0.0) for t in terms], axis=0).astype(jnp.bfloat16)
            )
            places.append(jnp.where(low_ids == low_of[row], 1.0, 0.0).astype(jnp.bfloat16))
        got = lax.dot_general(
            jnp.concatenate(spread, axis=1),
            jnp.concatenate(places, axis=1),
            (((1,), (1,)), ((), ())),
            preferred_element_type=jnp.float32,
        )
        grad[...] += sum(got[k * high : (k + 1) * high] for k in range(len(terms)))

    @pl.loop(0, clusters, unroll=4)
    def _(c):
        panels(c)


def finish(column_total, fwd_terms, adj_terms, params, weights, counts, high):
    clusters, part, width = fwd_terms[0].shape
    vmem = pl.BlockSpec(memory_space=pltpu.VMEM)
    first_clusters = pl.BlockSpec((clusters, part, width), lambda i: (0, 0, 0))
    field = jax.ShapeDtypeStruct((clusters, part // 2, 2 * width), jnp.float32)
    whole = lambda shape: pl.BlockSpec(shape, lambda i: (0,) * len(shape))
    terms = [*fwd_terms, *adj_terms]
    return pl.pallas_call(
        functools.partial(final_kernel, column_total, len(fwd_terms), len(adj_terms)),
        grid=(1,),
        in_specs=[first_clusters] * len(terms)
        + [whole(params.shape), whole(weights.shape), whole(counts.shape)],
        out_specs=[whole(field.shape), whole(field.shape), whole((high, width))],
        out_shape=[field, field, jax.ShapeDtypeStruct((high, width), jnp.float32)],
        compiler_params=pltpu.CompilerParams(vmem_limit_bytes=VMEM_BYTES),
        cost_estimate=pl.CostEstimate(flops=200_000_000, bytes_accessed=3_000_000, transcendentals=0),
    )(*terms, params, weights, counts)


def shards(
    forward_rhs,
    adjoint_rhs,
    far_clusters,
    far_ranks,
    far_left,
    far_right,
    near_clusters,
    near_blocks,
    panel_params,
    panel_weights,
    panel_counts,
):
    groups = lax.axis_size("clus")
    members = lax.axis_size("sub")
    clusters = forward_rhs.shape[0]
    total = clusters * groups
    column_total = forward_rhs.shape[1] * members
    evens = range(0, members, 2)

    def across(x):
        return [x if m == 0 else moved(x, 0, m) for m in evens]

    def both_cores(mine):
        pieces = []
        for x in mine:
            pieces += [x, moved(x, 0, 1)]
        return pieces

    tie = lax.optimization_barrier
    w_mine = across(adjoint_rhs)
    x_next, x_prev = moved(forward_rhs, -1, 0), moved(forward_rhs, 1, 0)
    factors = loaded(far_left, far_right, near_blocks)
    w_mine, factors = tie((w_mine, factors))
    left, right, near = factors
    w_pieces = both_cores(w_mine)
    w_pieces, x_next, x_prev = tie((w_pieces, x_next, x_prev))
    x_mine = [*across(forward_rhs), *across(x_next), *across(x_prev)]

    apply = functools.partial(
        apply_blocks, total=total, members=members, far_ids=far_clusters, ranks=far_ranks, near_ids=near_clusters
    )
    adj_parts = apply(True, pieces=w_pieces, first=left, second=right, near=near)
    adj_parts, x_mine = tie((adj_parts, x_mine))
    adj_core = [moved(adj_parts[m + 1], 0, 1) for m in evens]
    x_pieces = both_cores(x_mine)
    away = {
        m: (adj_parts[m] + adj_core[k]).astype(jnp.bfloat16) for k, m in enumerate(evens) if m
    }
    x_pieces, away = tie((x_pieces, away))
    sides = [moved(away[m][clusters:], 0, m) for m in away]
    own = [moved(away[m][:clusters], 0, m) for m in away]
    fwd_parts = apply(False, pieces=x_pieces, first=right, second=left, near=near)
    fwd_core = [moved(fwd_parts[m + 1], 0, 1) for m in evens]

    side = adj_parts[0][clusters:] + adj_core[0][clusters:]
    for s in sides:
        side = side + s.astype(jnp.float32)
    side = side.astype(jnp.bfloat16)
    ring = [moved(side[:clusters], 1, 0), moved(side[clusters:], -1, 0)]
    adj_terms = [adj_parts[0], adj_core[0], *own, *ring]

    fwd_terms = [fwd_parts[0], fwd_core[0]]
    for k, m in enumerate(evens):
        if m:
            fwd_terms.append(moved((fwd_parts[m] + fwd_core[k]).astype(jnp.bfloat16), 0, m))

    devices = groups * members
    forward_field, adjoint_field, spread = finish(
        column_total, fwd_terms, adj_terms, panel_params, panel_weights, panel_counts[None, :],
        PAR_DEV * devices // near_blocks.shape[-1],
    )
    pieces = lax.all_to_all(spread.reshape(devices, PAR_DEV), AXES, 0, 0, tiled=True)
    return forward_field, adjoint_field, jnp.sum(pieces, axis=0)


def solution(mesh):
    in_specs = (
        P("clus", "sub", None),
        P("clus", "sub", None),
        P(None, ("clus", "sub")),
        P(("clus", "sub")),
        P(("clus", "sub"), None, None, None),
        P(("clus", "sub"), None, None, None),
        P(None, ("clus", "sub")),
        P(("clus", "sub"), None, None, None),
        P(None, "clus"),
        P(None, "clus"),
        P("clus"),
    )
    out_specs = (P("clus", "sub", None), P("clus", "sub", None), P(("clus", "sub")))
    return jax.shard_map(shards, mesh=mesh, in_specs=in_specs, out_specs=out_specs, check_vma=False)
```

```python
import functools

import jax
import jax.numpy as jnp
from jax import lax
from jax.experimental import pallas as pl
from jax.experimental.pallas import tpu as pltpu
from jax.sharding import PartitionSpec as P

PAR_DEV = 128
AXES = ("clus", "sub")
FAR_UNROLL = 128
NEAR_UNROLL = 32
VMEM_BYTES = 40 * 1024 * 1024
LOAD_BYTES = 46 * 1024 * 1024


def moved(x, by, mask):
    groups, members = lax.axis_size("clus"), lax.axis_size("sub")
    pairs = [
        (g * members + s, ((g + by) % groups) * members + (s ^ mask))
        for g in range(groups)
        for s in range(members)
    ]
    return lax.ppermute(x, AXES, pairs)


def wide_place(cluster, row, clusters, total):
    first = row - lax.rem(row, clusters)
    place = lax.rem(cluster - first + total, total)
    return jnp.where(place >= 2 * clusters, place - (total - 3 * clusters), place)


def block_kernel(transposed, total, members, *refs):
    tables_in = refs[:3]
    pieces = refs[3 : 3 + members]
    first, second, near = refs[3 + members : 6 + members]
    outs = refs[6 + members : 6 + 2 * members]
    lhs, coeffs, far_ids, ranks, near_ids, sems = refs[6 + 2 * members :]
    tables = (far_ids, ranks, near_ids)
    copies = [pltpu.make_async_copy(a, b, sems.at[i]) for i, (a, b) in enumerate(zip(tables_in, tables))]
    for copy in copies:
        copy.start()
    field_clusters, height, _ = pieces[0].shape
    clusters = field_clusters if transposed else field_clusters // 3
    far, _, rank, width = first.shape
    near_total = near.shape[0]
    rows = lhs.shape[1]
    part = 2 * height
    for out in outs:
        out[...] = jnp.zeros_like(out)

    @pl.loop(0, field_clusters, unroll=4)
    def _(c):
        left, right = [], []
        for piece in pieces:
            x = piece[c].astype(jnp.float32)
            re, im = x[:, :width], x[:, width:]
            left += [re, im]
            right += [-im, re]
        both = [jnp.concatenate(left, axis=0), jnp.concatenate(right, axis=0)]
        lhs[c] = jnp.concatenate(both, axis=1).astype(jnp.bfloat16)

    for copy in copies:
        copy.wait()

    def add(place, value):
        for i, out in enumerate(outs):
            out[place] += value[i * part : (i + 1) * part]

    def places(ids, b):
        row = ids[0, b]
        column = wide_place(ids[1, b], row, clusters, total)
        row = lax.rem(row, clusters)
        return (row, column) if transposed else (column, row)

    rank_ids = lax.broadcasted_iota(jnp.int32, (rows, 2 * rank), 1)
    rank_ids = jnp.where(rank_ids >= rank, rank_ids - rank, rank_ids)

    far_unroll = min(FAR_UNROLL, far)
    near_unroll = min(NEAR_UNROLL, near_total)

    @pl.loop(0, far // far_unroll)
    def _(t):
        for i in range(far_unroll):
            b = t * far_unroll + i
            re, im = first[b, 0], first[b, 1]
            factor = jnp.concatenate(
                [jnp.concatenate([re, im], axis=1), jnp.concatenate([-im, re], axis=1)], axis=0
            )
            coeff = lax.dot_general(
                lhs[places(far_ids, b)[0]],
                factor,
                (((1,), (1,)), ((), ())),
                preferred_element_type=jnp.float32,
            )
            coeffs[i] = jnp.where(rank_ids < ranks[b], coeff, 0.0).astype(jnp.bfloat16)
        for i in range(far_unroll):
            b = t * far_unroll + i
            value = jnp.dot(
                coeffs[i], second[b].reshape(2 * rank, width), preferred_element_type=jnp.float32
            )
            add(places(far_ids, b)[1], value)

    @pl.loop(0, near_total // near_unroll)
    def _(t):
        for i in range(near_unroll):
            b = t * near_unroll + i
            source, place = places(near_ids, b)
            if transposed:
                value = jnp.dot(
                    lhs[source],
                    near[b].reshape(2 * width, width),
                    preferred_element_type=jnp.float32,
                )
            else:
                value = lax.dot_general(
                    lhs[source],
                    jnp.concatenate([near[b, 0], near[b, 1]], axis=1),
                    (((1,), (1,)), ((), ())),
                    preferred_element_type=jnp.float32,
                )
            add(place, value)


def apply_blocks(transposed, total, members, far_ids, ranks, near_ids, pieces, first, second, near):
    field_clusters, height, double = pieces[0].shape
    out_clusters = 3 * field_clusters if transposed else field_clusters // 3
    rows = members * 2 * height
    rank, width = first.shape[2:]
    anywhere = pl.BlockSpec(memory_space=pl.ANY)
    vmem = pl.BlockSpec(memory_space=pltpu.VMEM)
    tables = (far_ids, ranks, near_ids)
    flops = 2 * rows * (first.shape[0] * 2 * 2 * rank * 2 * width + near.shape[0] * 2 * width * width)
    return pl.pallas_call(
        functools.partial(block_kernel, transposed, total, members),
        in_specs=[anywhere] * 3 + [vmem] * (len(pieces) + 3),
        out_specs=[vmem] * members,
        out_shape=[
            jax.ShapeDtypeStruct((out_clusters, 2 * height, width), jnp.float32)
        ] * members,
        scratch_shapes=[
            pltpu.VMEM((field_clusters, rows, double), jnp.bfloat16),
            pltpu.VMEM((min(FAR_UNROLL, first.shape[0]), rows, 2 * rank), jnp.bfloat16),
            *[pltpu.SMEM(t.shape, t.dtype) for t in tables],
            pltpu.SemaphoreType.DMA((len(tables),)),
        ],
        compiler_params=pltpu.CompilerParams(vmem_limit_bytes=VMEM_BYTES),
        cost_estimate=pl.CostEstimate(flops=flops, bytes_accessed=20_000_000, transcendentals=0),
    )(*tables, *pieces, first, second, near)


def load_kernel(parts, *refs):
    count = (len(refs) - 1) // 2
    sources, targets, sems = refs[:count], refs[count : 2 * count], refs[2 * count]
    copies = []
    for i, (source, target) in enumerate(zip(sources, targets)):
        length = source.shape[0] // parts
        for k in range(parts):
            at = pl.ds(k * length, length)
            copies.append(pltpu.make_async_copy(source.at[at], target.at[at], sems.at[i, k]))
    for copy in copies:
        copy.start()
    for copy in copies:
        copy.wait()


def loaded(*arrays):
    parts = 4
    return pl.pallas_call(
        functools.partial(load_kernel, parts),
        in_specs=[pl.BlockSpec(memory_space=pltpu.HBM)] * len(arrays),
        out_specs=[pl.BlockSpec(memory_space=pltpu.VMEM)] * len(arrays),
        out_shape=[jax.ShapeDtypeStruct(a.shape, a.dtype) for a in arrays],
        scratch_shapes=[pltpu.SemaphoreType.DMA((len(arrays), parts))],
        compiler_params=pltpu.CompilerParams(vmem_limit_bytes=LOAD_BYTES),
        cost_estimate=pl.CostEstimate(flops=0, bytes_accessed=12_000_000, transcendentals=0),
    )(*arrays)


def table_kernel(params, weights, counts, spread, places):
    slots, panels = params.shape
    high, width = spread.shape[0], places.shape[0]
    shift = width.bit_length() - 1
    high_ids = lax.broadcasted_iota(jnp.int32, (high, width), 0)
    low_ids = lax.broadcasted_iota(jnp.int32, (width, width), 0)
    slot_ids = lax.broadcasted_iota(jnp.int32, (slots, width), 0)
    for c in range(panels // width):
        at = slice(c * width, (c + 1) * width)
        value = jnp.where(slot_ids < counts[:, at], weights[:, at], 0.0)
        ids = params[:, at]
        high_of, low_of = ids >> shift, ids & (width - 1)
        for m in range(slots):
            row = slice(m, m + 1)
            to = slice((c * slots + m) * width, (c * slots + m + 1) * width)
            spread[:, to] = jnp.where(high_ids == high_of[row], value[row], 0.0)
            places[:, to] = jnp.where(low_ids == low_of[row], 1.0, 0.0).astype(jnp.bfloat16)


def gradient_tables(params, weights, counts, high, width):
    vmem = pl.BlockSpec(memory_space=pltpu.VMEM)
    entries = params.size
    return pl.pallas_call(
        table_kernel,
        in_specs=[vmem] * 3,
        out_specs=[vmem] * 2,
        out_shape=[
            jax.ShapeDtypeStruct((high, entries), jnp.float32),
            jax.ShapeDtypeStruct((width, entries), jnp.bfloat16),
        ],
        compiler_params=pltpu.CompilerParams(vmem_limit_bytes=VMEM_BYTES),
        cost_estimate=pl.CostEstimate(flops=0, bytes_accessed=8_000_000, transcendentals=0),
    )(params, weights, counts)


def final_kernel(column_total, n_fwd, n_adj, *refs):
    fwd_terms = refs[:n_fwd]
    adj_terms = refs[n_fwd : n_fwd + n_adj]
    spread, places, fwd_out, adj_out, grad, scaled = refs[n_fwd + n_adj :]
    clusters, height, _ = fwd_out.shape
    high, width = grad.shape
    entries = spread.shape[1] // clusters
    slots = entries // width
    for c in range(clusters):
        fwd = sum(t[c].astype(jnp.float32) for t in fwd_terms)
        adj = sum(t[c].astype(jnp.float32) for t in adj_terms)
        for out, value in ((fwd_out, fwd), (adj_out, adj)):
            out[c, :, :width] = value[:height]
            out[c, :, width:] = value[height:]
        product = fwd * adj
        sens = jnp.sum(product[:height] - product[height:], axis=0, keepdims=True) / column_total
        at = slice(c * entries, (c + 1) * entries)
        value = spread[:, at] * jnp.concatenate([sens] * slots, axis=1)
        top = value.astype(jnp.bfloat16)
        scaled[:high, at] = top
        scaled[high:, at] = (value - top.astype(jnp.float32)).astype(jnp.bfloat16)
    got = lax.dot_general(
        scaled[...], places[...], (((1,), (1,)), ((), ())), preferred_element_type=jnp.float32
    )
    grad[...] = got[:high] + got[high:]


def finish(column_total, fwd_terms, adj_terms, spread, places):
    clusters, part, width = fwd_terms[0].shape
    high = spread.shape[0]
    first_clusters = pl.BlockSpec((clusters, part, width), lambda i: (0, 0, 0))
    field = jax.ShapeDtypeStruct((clusters, part // 2, 2 * width), jnp.float32)
    whole = lambda shape: pl.BlockSpec(shape, lambda i: (0,) * len(shape))
    terms = [*fwd_terms, *adj_terms]
    return pl.pallas_call(
        functools.partial(final_kernel, column_total, len(fwd_terms), len(adj_terms)),
        grid=(1,),
        in_specs=[first_clusters] * len(terms)
        + [pl.BlockSpec(memory_space=pltpu.VMEM)] * 2,
        out_specs=[whole(field.shape), whole(field.shape), whole((high, width))],
        out_shape=[field, field, jax.ShapeDtypeStruct((high, width), jnp.float32)],
        scratch_shapes=[pltpu.VMEM((2 * high, spread.shape[1]), jnp.bfloat16)],
        compiler_params=pltpu.CompilerParams(vmem_limit_bytes=VMEM_BYTES),
        cost_estimate=pl.CostEstimate(flops=200_000_000, bytes_accessed=3_000_000, transcendentals=0),
    )(*terms, spread, places)


def shards(
    forward_rhs,
    adjoint_rhs,
    far_clusters,
    far_ranks,
    far_left,
    far_right,
    near_clusters,
    near_blocks,
    panel_params,
    panel_weights,
    panel_counts,
):
    groups = lax.axis_size("clus")
    members = lax.axis_size("sub")
    clusters = forward_rhs.shape[0]
    total = clusters * groups
    column_total = forward_rhs.shape[1] * members
    evens = range(0, members, 2)

    def across(x):
        return [x if m == 0 else moved(x, 0, m) for m in evens]

    def both_cores(mine):
        pieces = []
        for x in mine:
            pieces += [x, moved(x, 0, 1)]
        return pieces

    tie = lax.optimization_barrier
    w_mine = across(adjoint_rhs)
    x_prev = moved(forward_rhs, 1, 0)
    x_next = moved(forward_rhs, -1, 0)
    left, right, near, w_mine[0] = loaded(far_left, far_right, near_blocks, adjoint_rhs)
    x_own = across(forward_rhs)
    w_mine, x_own, left, right, near = tie((w_mine, x_own, left, right, near))
    w_pieces = both_cores(w_mine)
    x_near = jnp.concatenate([x_next, x_prev], axis=0)
    w_pieces, x_near = tie((w_pieces, x_near))
    x_near = across(x_near)
    x_mine = [jnp.concatenate(pair, axis=0) for pair in zip(x_own, x_near)]

    apply = functools.partial(
        apply_blocks, total=total, members=members, far_ids=far_clusters, ranks=far_ranks, near_ids=near_clusters
    )
    adj_parts = apply(True, pieces=w_pieces, first=left, second=right, near=near)
    adj_parts, x_mine = tie((adj_parts, x_mine))
    adj_core = [moved(adj_parts[m + 1], 0, 1) for m in evens]
    x_pieces = both_cores(x_mine)
    away = {
        m: (adj_parts[m] + adj_core[k]).astype(jnp.bfloat16) for k, m in enumerate(evens) if m
    }
    x_pieces, away = tie((x_pieces, away))
    sides = [moved(away[m][clusters:], 0, m) for m in away]
    own = [moved(away[m][:clusters], 0, m) for m in away]
    fwd_parts = apply(False, pieces=x_pieces, first=right, second=left, near=near)
    fwd_parts, sides = tie((fwd_parts, sides))
    fwd_core = [moved(fwd_parts[m + 1], 0, 1) for m in evens]

    side = adj_parts[0][clusters:] + adj_core[0][clusters:]
    for s in sides:
        side = side + s.astype(jnp.float32)
    side = side.astype(jnp.bfloat16)
    panel_params, side = tie((panel_params, side))
    spread, places = gradient_tables(
        panel_params, panel_weights, panel_counts[None, :],
        PAR_DEV * groups * members // near_blocks.shape[-1], near_blocks.shape[-1],
    )
    ring = [moved(side[:clusters], 1, 0), moved(side[clusters:], -1, 0)]
    adj_terms = [adj_parts[0], adj_core[0], *own, *ring]

    fwd_terms = [fwd_parts[0], fwd_core[0]]
    for k, m in enumerate(evens):
        if m:
            fwd_terms.append(moved((fwd_parts[m] + fwd_core[k]).astype(jnp.bfloat16), 0, m))

    devices = groups * members
    forward_field, adjoint_field, grad = finish(column_total, fwd_terms, adj_terms, spread, places)
    pieces = lax.all_to_all(grad.reshape(devices, PAR_DEV), AXES, 0, 0, tiled=True)
    return forward_field, adjoint_field, jnp.sum(pieces, axis=0)


def solution(mesh):
    in_specs = (
        P("clus", "sub", None),
        P("clus", "sub", None),
        P(None, ("clus", "sub")),
        P(("clus", "sub")),
        P(("clus", "sub"), None, None, None),
        P(("clus", "sub"), None, None, None),
        P(None, ("clus", "sub")),
        P(("clus", "sub"), None, None, None),
        P(None, "clus"),
        P(None, "clus"),
        P("clus"),
    )
    out_specs = (P("clus", "sub", None), P("clus", "sub", None), P(("clus", "sub")))
    return jax.shard_map(shards, mesh=mesh, in_specs=in_specs, out_specs=out_specs, check_vma=False)
```

```python
import functools

import jax
import jax.numpy as jnp
from jax import lax
from jax.experimental import pallas as pl
from jax.experimental.pallas import tpu as pltpu
from jax.sharding import PartitionSpec as P

PAR_DEV = 128
AXES = ("clus", "sub")
LOADS = 4
VMEM_BYTES = 40 * 1024 * 1024
LOAD_BYTES = 46 * 1024 * 1024


def moved(x, by, mask):
    groups, members = lax.axis_size("clus"), lax.axis_size("sub")
    pairs = [
        (g * members + s, ((g + by) % groups) * members + (s ^ mask))
        for g in range(groups)
        for s in range(members)
    ]
    return lax.ppermute(x, AXES, pairs)


def round_ring(x):
    groups, members = lax.axis_size("clus"), lax.axis_size("sub")
    pairs = [
        (g * members + s, ((g + 1 - 2 * (s % 2)) % groups) * members + s)
        for g in range(groups)
        for s in range(members)
    ]
    return lax.ppermute(x, AXES, pairs)


def wide_place(cluster, row, clusters, total, previous_first):
    first = row - lax.rem(row, clusters)
    place = lax.rem(cluster - first + total, total)
    near = lax.rem(place, clusters)
    following = jnp.where(previous_first, 2 * clusters, clusters)
    preceding = 3 * clusters - following
    side = jnp.where(place < 2 * clusters, following, preceding)
    return jnp.where(place < clusters, place, side + near)


def block_kernel(transposed, total, members, *refs):
    tables_in = refs[:3]
    count = members if transposed else members + 2
    fields = refs[3 : 3 + count]
    first, second, near, out = refs[3 + count : -6]
    lhs, coeffs, far_ids, ranks, near_ids, sems = refs[-6:]
    tables = (far_ids, ranks, near_ids)
    copies = [pltpu.make_async_copy(a, b, sems.at[i]) for i, (a, b) in enumerate(zip(tables_in, tables))]
    for copy in copies:
        copy.start()

    height = fields[0].shape[1]
    clusters = fields[0].shape[0]
    far, _, rank, width = first.shape
    near_total = near.shape[0]
    rows = lhs.shape[1]
    core = lax.rem(lax.axis_index("sub"), 2)
    previous_first = core == (1 if transposed else 0)
    out[...] = jnp.zeros_like(out)

    def build(place, pieces):
        left, right = [], []
        for piece in pieces:
            x = piece.astype(jnp.float32)
            re, im = x[:, :width], x[:, width:]
            left += [re, im]
            right += [-im, re]
        both = [jnp.concatenate(left, axis=0), jnp.concatenate(right, axis=0)]
        lhs[place] = jnp.concatenate(both, axis=1).astype(jnp.bfloat16)

    @pl.loop(0, clusters, unroll=4)
    def _(c):
        build(c, [field[c] for field in fields[:members]])

    if not transposed:

        @pl.loop(0, clusters, unroll=4)
        def _(c):
            here, there = fields[members:]
            build(clusters + c, [here[m * clusters + c] for m in range(members)])
            build(2 * clusters + c, [there[(m ^ 1) * clusters + c] for m in range(members)])

    for copy in copies:
        copy.wait()

    def places(ids, b):
        row = ids[0, b]
        column = wide_place(ids[1, b], row, clusters, total, previous_first)
        row = lax.rem(row, clusters)
        return (row, column) if transposed else (column, row)

    rank_ids = lax.broadcasted_iota(jnp.int32, (rows, 2 * rank), 1)
    rank_ids = jnp.where(rank_ids >= rank, rank_ids - rank, rank_ids)

    for b in range(far):
        re, im = first[b, 0], first[b, 1]
        factor = jnp.concatenate(
            [jnp.concatenate([re, im], axis=1), jnp.concatenate([-im, re], axis=1)], axis=0
        )
        coeff = lax.dot_general(
            lhs[places(far_ids, b)[0]],
            factor,
            (((1,), (1,)), ((), ())),
            preferred_element_type=jnp.float32,
        )
        coeffs[b] = jnp.where(rank_ids < ranks[b], coeff, 0.0).astype(jnp.bfloat16)
    for b in range(far):
        out[places(far_ids, b)[1]] += jnp.dot(
            coeffs[b], second[b].reshape(2 * rank, width), preferred_element_type=jnp.float32
        )
    for b in range(near_total):
        source, place = places(near_ids, b)
        if transposed:
            value = jnp.dot(
                lhs[source], near[b].reshape(2 * width, width), preferred_element_type=jnp.float32
            )
        else:
            value = lax.dot_general(
                lhs[source],
                jnp.concatenate([near[b, 0], near[b, 1]], axis=1),
                (((1,), (1,)), ((), ())),
                preferred_element_type=jnp.float32,
            )
        out[place] += value


def apply_blocks(transposed, total, members, far_ids, ranks, near_ids, fields, first, second, near):
    clusters, height, double = fields[0].shape
    rows = members * 2 * height
    rank, width = first.shape[2:]
    anywhere = pl.BlockSpec(memory_space=pl.ANY)
    vmem = pl.BlockSpec(memory_space=pltpu.VMEM)
    tables = (far_ids, ranks, near_ids)
    flops = 2 * rows * (first.shape[0] * 2 * 2 * rank * 2 * width + near.shape[0] * 2 * width * width)
    return pl.pallas_call(
        functools.partial(block_kernel, transposed, total, members),
        in_specs=[anywhere] * 3 + [vmem] * (len(fields) + 3),
        out_specs=vmem,
        out_shape=jax.ShapeDtypeStruct((clusters * (3 if transposed else 1), rows, width), jnp.float32),
        scratch_shapes=[
            pltpu.VMEM((clusters * (1 if transposed else 3), rows, double), jnp.bfloat16),
            pltpu.VMEM((first.shape[0], rows, 2 * rank), jnp.bfloat16),
            *[pltpu.SMEM(t.shape, t.dtype) for t in tables],
            pltpu.SemaphoreType.DMA((len(tables),)),
        ],
        compiler_params=pltpu.CompilerParams(vmem_limit_bytes=VMEM_BYTES),
        cost_estimate=pl.CostEstimate(flops=flops, bytes_accessed=20_000_000, transcendentals=0),
    )(*tables, *fields, first, second, near)


def load_kernel(parts, *refs):
    count = (len(refs) - 1) // 2
    sources, targets, sems = refs[:count], refs[count : 2 * count], refs[2 * count]
    copies = []
    for i, (source, target) in enumerate(zip(sources, targets)):
        length = source.shape[0] // parts
        for k in range(parts):
            at = pl.ds(k * length, length)
            copies.append(pltpu.make_async_copy(source.at[at], target.at[at], sems.at[i, k]))
    for copy in copies:
        copy.start()
    for copy in copies:
        copy.wait()


def loaded(*arrays):
    return pl.pallas_call(
        functools.partial(load_kernel, LOADS),
        in_specs=[pl.BlockSpec(memory_space=pltpu.HBM)] * len(arrays),
        out_specs=[pl.BlockSpec(memory_space=pltpu.VMEM)] * len(arrays),
        out_shape=[jax.ShapeDtypeStruct(a.shape, a.dtype) for a in arrays],
        scratch_shapes=[pltpu.SemaphoreType.DMA((len(arrays), LOADS))],
        compiler_params=pltpu.CompilerParams(vmem_limit_bytes=LOAD_BYTES),
        cost_estimate=pl.CostEstimate(flops=0, bytes_accessed=12_000_000, transcendentals=0),
    )(*arrays)


def table_kernel(params, weights, counts, spread, places):
    slots, panels = params.shape
    high, width = spread.shape[0], places.shape[0]
    shift = width.bit_length() - 1
    high_ids = lax.broadcasted_iota(jnp.int32, (high, width), 0)
    low_ids = lax.broadcasted_iota(jnp.int32, (width, width), 0)
    slot_ids = lax.broadcasted_iota(jnp.int32, (slots, width), 0)
    for c in range(panels // width):
        at = slice(c * width, (c + 1) * width)
        value = jnp.where(slot_ids < counts[:, at], weights[:, at], 0.0)
        ids = params[:, at]
        high_of, low_of = ids >> shift, ids & (width - 1)
        for m in range(slots):
            row = slice(m, m + 1)
            to = slice((c * slots + m) * width, (c * slots + m + 1) * width)
            spread[:, to] = jnp.where(high_ids == high_of[row], value[row], 0.0)
            places[:, to] = jnp.where(low_ids == low_of[row], 1.0, 0.0).astype(jnp.bfloat16)


def gradient_tables(params, weights, counts, high, width):
    vmem = pl.BlockSpec(memory_space=pltpu.VMEM)
    entries = params.size
    return pl.pallas_call(
        table_kernel,
        in_specs=[vmem] * 3,
        out_specs=[vmem] * 2,
        out_shape=[
            jax.ShapeDtypeStruct((high, entries), jnp.float32),
            jax.ShapeDtypeStruct((width, entries), jnp.bfloat16),
        ],
        compiler_params=pltpu.CompilerParams(vmem_limit_bytes=VMEM_BYTES),
        cost_estimate=pl.CostEstimate(flops=0, bytes_accessed=8_000_000, transcendentals=0),
    )(params, weights, counts)


def final_kernel(column_total, n_fwd, n_adj, *refs):
    fwd_terms = refs[:n_fwd]
    adj_terms = refs[n_fwd : n_fwd + n_adj]
    spread, places, fwd_out, adj_out, grad, scaled = refs[n_fwd + n_adj :]
    clusters, height, _ = fwd_out.shape
    high, width = grad.shape
    entries = spread.shape[1] // clusters
    slots = entries // width
    for c in range(clusters):
        fwd = sum(t[c, : 2 * height].astype(jnp.float32) for t in fwd_terms)
        adj = sum(t[c, : 2 * height].astype(jnp.float32) for t in adj_terms)
        for out, value in ((fwd_out, fwd), (adj_out, adj)):
            out[c, :, :width] = value[:height]
            out[c, :, width:] = value[height:]
        product = fwd * adj
        sens = jnp.sum(product[:height] - product[height:], axis=0, keepdims=True) / column_total
        at = slice(c * entries, (c + 1) * entries)
        value = spread[:, at] * jnp.concatenate([sens] * slots, axis=1)
        top = value.astype(jnp.bfloat16)
        scaled[:high, at] = top
        scaled[high:, at] = (value - top.astype(jnp.float32)).astype(jnp.bfloat16)
    got = lax.dot_general(
        scaled[...], places[...], (((1,), (1,)), ((), ())), preferred_element_type=jnp.float32
    )
    grad[...] = got[:high] + got[high:]


def finish(column_total, shape, fwd_terms, adj_terms, spread, places):
    high, width = spread.shape[0], places.shape[0]
    vmem = pl.BlockSpec(memory_space=pltpu.VMEM)
    terms = [*fwd_terms, *adj_terms]
    field = jax.ShapeDtypeStruct(shape, jnp.float32)
    return pl.pallas_call(
        functools.partial(final_kernel, column_total, len(fwd_terms), len(adj_terms)),
        in_specs=[vmem] * (len(terms) + 2),
        out_specs=[vmem] * 3,
        out_shape=[field, field, jax.ShapeDtypeStruct((high, width), jnp.float32)],
        scratch_shapes=[pltpu.VMEM((2 * high, spread.shape[1]), jnp.bfloat16)],
        compiler_params=pltpu.CompilerParams(vmem_limit_bytes=VMEM_BYTES),
        cost_estimate=pl.CostEstimate(flops=200_000_000, bytes_accessed=3_000_000, transcendentals=0),
    )(*terms, spread, places)


def shards(
    forward_rhs,
    adjoint_rhs,
    far_clusters,
    far_ranks,
    far_left,
    far_right,
    near_clusters,
    near_blocks,
    panel_params,
    panel_weights,
    panel_counts,
):
    groups = lax.axis_size("clus")
    members = lax.axis_size("sub")
    clusters = forward_rhs.shape[0]
    total = clusters * groups
    column_total = forward_rhs.shape[1] * members
    evens = range(0, members, 2)

    height = forward_rhs.shape[1]
    part, rows = 2 * height, 2 * height * members
    tie = lax.optimization_barrier

    w_mine = [adjoint_rhs if m == 0 else moved(adjoint_rhs, 0, m) for m in evens]
    x_chip = [forward_rhs, moved(forward_rhs, 0, 1)]
    x_ring = jnp.concatenate([round_ring(x) for x in x_chip], axis=0)
    x_own = [forward_rhs if m == 0 else moved(forward_rhs, 0, m) for m in evens]
    left, right, near = loaded(far_left, far_right, near_blocks)
    w_mine, x_own, left, right, near = tie((w_mine, x_own, left, right, near))
    w_pieces = [x for m in range(0, members, 2) for x in (w_mine[m // 2], moved(w_mine[m // 2], 0, 1))]
    x_pieces = [*x_chip]
    for x in x_own[1:]:
        x_pieces += [x, moved(x, 0, 1)]
    w_pieces, x_ring = tie((w_pieces, x_ring))
    x_side = [x_ring if m == 0 else moved(x_ring, 0, m) for m in evens]

    apply = functools.partial(
        apply_blocks, total=total, members=members, far_ids=far_clusters, ranks=far_ranks, near_ids=near_clusters
    )
    adj = apply(True, fields=w_pieces, first=left, second=right, near=near)
    x_side, _ = tie((x_side, adj))
    x_here = jnp.concatenate(x_side, axis=0)
    x_there = moved(x_here, 0, 1)

    def rows_of(field, m):
        return field[:, m * part : (m + 2) * part]

    def chip_sums(m):
        given = moved(rows_of(adj[2 * clusters :], m).astype(jnp.bfloat16), 0, 1).astype(jnp.float32)
        given = jnp.concatenate([given[:, part:], given[:, :part]], axis=1)
        return rows_of(adj[clusters : 2 * clusters], m) + given

    sides = [moved(chip_sums(m).astype(jnp.bfloat16), 0, m) for m in evens if m]
    odd_rows = [adj[:clusters, m * part : (m + 1) * part] for m in range(1, members, 2)]
    x_there, odd_rows = tie((x_there, odd_rows))
    adj_core = moved(jnp.concatenate(odd_rows, axis=1), 0, 1)
    fwd = apply(False, fields=[*x_pieces, x_here, x_there], first=right, second=left, near=near)
    fwd, sides, adj_core = tie((fwd, sides, adj_core))

    def own_sum(field, core_part, m):
        k = m // 2
        return field[:clusters, m * part : (m + 1) * part] + core_part[:, k * part : (k + 1) * part]

    fwd_core = moved(
        jnp.concatenate([fwd[:, m * part : (m + 1) * part] for m in range(1, members, 2)], axis=1), 0, 1
    )
    side = chip_sums(0)
    for s in sides:
        side = side + s.astype(jnp.float32)
    side = side.astype(jnp.bfloat16)
    panel_params, side = tie((panel_params, side))
    spread, places = gradient_tables(
        panel_params, panel_weights, panel_counts[None, :],
        PAR_DEV * groups * members // near_blocks.shape[-1], near_blocks.shape[-1],
    )
    ring = round_ring(side)
    own = [moved(own_sum(adj, adj_core, m).astype(jnp.bfloat16), 0, m) for m in evens if m]
    over = [moved(own_sum(fwd, fwd_core, m).astype(jnp.bfloat16), 0, m) for m in evens if m]
    ring, over = tie((ring, over))
    ring_core = moved(ring[:, part:], 0, 1)
    forward_field, adjoint_field, grad = finish(
        column_total, forward_rhs.shape, [fwd, fwd_core, *over], [adj, adj_core, *own, ring, ring_core], spread, places
    )
    devices = groups * members
    pieces = lax.all_to_all(grad.reshape(devices, PAR_DEV), AXES, 0, 0, tiled=True)
    return forward_field, adjoint_field, jnp.sum(pieces, axis=0)


def solution(mesh):
    in_specs = (
        P("clus", "sub", None),
        P("clus", "sub", None),
        P(None, ("clus", "sub")),
        P(("clus", "sub")),
        P(("clus", "sub"), None, None, None),
        P(("clus", "sub"), None, None, None),
        P(None, ("clus", "sub")),
        P(("clus", "sub"), None, None, None),
        P(None, "clus"),
        P(None, "clus"),
        P("clus"),
    )
    out_specs = (P("clus", "sub", None), P("clus", "sub", None), P(("clus", "sub")))
    return jax.shard_map(shards, mesh=mesh, in_specs=in_specs, out_specs=out_specs, check_vma=False)
```

```python
import functools

import jax
import jax.numpy as jnp
from jax import lax
from jax.experimental import pallas as pl
from jax.experimental.pallas import tpu as pltpu
from jax.sharding import PartitionSpec as P

PAR_DEV = 128
AXES = ("clus", "sub")
LOADS = 4
VMEM_BYTES = 40 * 1024 * 1024
LOAD_BYTES = 46 * 1024 * 1024


def moved(x, by, mask):
    groups, members = lax.axis_size("clus"), lax.axis_size("sub")
    pairs = [
        (g * members + s, ((g + by) % groups) * members + (s ^ mask))
        for g in range(groups)
        for s in range(members)
    ]
    return lax.ppermute(x, AXES, pairs)


def round_ring(x):
    groups, members = lax.axis_size("clus"), lax.axis_size("sub")
    pairs = [
        (g * members + s, ((g + 1 - 2 * (s % 2)) % groups) * members + s)
        for g in range(groups)
        for s in range(members)
    ]
    return lax.ppermute(x, AXES, pairs)


def wide_place(cluster, row, clusters, total, previous_first):
    first = row - lax.rem(row, clusters)
    place = lax.rem(cluster - first + total, total)
    near = lax.rem(place, clusters)
    following = jnp.where(previous_first, 2 * clusters, clusters)
    preceding = 3 * clusters - following
    side = jnp.where(place < 2 * clusters, following, preceding)
    return jnp.where(place < clusters, place, side + near)


def block_kernel(transposed, total, members, *refs):
    tables_in = refs[:3]
    count = members if transposed else members + 2
    fields = refs[3 : 3 + count]
    first, second, near, out, *give = refs[3 + count : -6]
    lhs, coeffs, far_ids, ranks, near_ids, sems = refs[-6:]
    tables = (far_ids, ranks, near_ids)
    copies = [pltpu.make_async_copy(a, b, sems.at[i]) for i, (a, b) in enumerate(zip(tables_in, tables))]
    for copy in copies:
        copy.start()

    height = fields[0].shape[1]
    clusters = fields[0].shape[0]
    far, _, rank, width = first.shape
    near_total = near.shape[0]
    rows = lhs.shape[1]
    core = lax.rem(lax.axis_index("sub"), 2)
    previous_first = core == (1 if transposed else 0)
    out[...] = jnp.zeros_like(out)

    def build(place, pieces):
        left, right = [], []
        for piece in pieces:
            x = piece.astype(jnp.float32)
            re, im = x[:, :width], x[:, width:]
            left += [re, im]
            right += [-im, re]
        both = [jnp.concatenate(left, axis=0), jnp.concatenate(right, axis=0)]
        lhs[place] = jnp.concatenate(both, axis=1).astype(jnp.bfloat16)

    @pl.loop(0, clusters, unroll=4)
    def _(c):
        build(c, [field[c] for field in fields[:members]])

    if not transposed:

        @pl.loop(0, clusters, unroll=4)
        def _(c):
            here, there = fields[members:]
            build(clusters + c, [here[m * clusters + c] for m in range(members)])
            build(2 * clusters + c, [there[(m ^ 1) * clusters + c] for m in range(members)])

    for copy in copies:
        copy.wait()

    def places(ids, b):
        row = ids[0, b]
        column = wide_place(ids[1, b], row, clusters, total, previous_first)
        row = lax.rem(row, clusters)
        return (row, column) if transposed else (column, row)

    rank_ids = lax.broadcasted_iota(jnp.int32, (rows, 2 * rank), 1)
    rank_ids = jnp.where(rank_ids >= rank, rank_ids - rank, rank_ids)

    for b in range(far):
        re, im = first[b, 0], first[b, 1]
        factor = jnp.concatenate(
            [jnp.concatenate([re, im], axis=1), jnp.concatenate([-im, re], axis=1)], axis=0
        )
        coeff = lax.dot_general(
            lhs[places(far_ids, b)[0]],
            factor,
            (((1,), (1,)), ((), ())),
            preferred_element_type=jnp.float32,
        )
        coeffs[b] = jnp.where(rank_ids < ranks[b], coeff, 0.0).astype(jnp.bfloat16)
    for b in range(far):
        out[places(far_ids, b)[1]] += jnp.dot(
            coeffs[b], second[b].reshape(2 * rank, width), preferred_element_type=jnp.float32
        )
    for b in range(near_total):
        source, place = places(near_ids, b)
        if transposed:
            value = jnp.dot(
                lhs[source], near[b].reshape(2 * width, width), preferred_element_type=jnp.float32
            )
        else:
            value = lax.dot_general(
                lhs[source],
                jnp.concatenate([near[b, 0], near[b, 1]], axis=1),
                (((1,), (1,)), ((), ())),
                preferred_element_type=jnp.float32,
            )
        out[place] += value
    part = 2 * height
    for k, half in enumerate(give):
        rows_here = out[2 * clusters :, 2 * k * part : (2 * k + 2) * part]
        half[...] = jnp.concatenate([rows_here[:, part:], rows_here[:, :part]], axis=1).astype(half.dtype)


def apply_blocks(transposed, total, members, far_ids, ranks, near_ids, fields, first, second, near):
    clusters, height, double = fields[0].shape
    rows = members * 2 * height
    rank, width = first.shape[2:]
    anywhere = pl.BlockSpec(memory_space=pl.ANY)
    vmem = pl.BlockSpec(memory_space=pltpu.VMEM)
    tables = (far_ids, ranks, near_ids)
    give = jax.ShapeDtypeStruct((clusters, 4 * height, width), jnp.bfloat16)
    gives = [give] * (members // 2) if transposed else []
    flops = 2 * rows * (first.shape[0] * 2 * 2 * rank * 2 * width + near.shape[0] * 2 * width * width)
    return pl.pallas_call(
        functools.partial(block_kernel, transposed, total, members),
        in_specs=[anywhere] * 3 + [vmem] * (len(fields) + 3),
        out_specs=[vmem] * (1 + len(gives)),
        out_shape=[
            jax.ShapeDtypeStruct((clusters * (3 if transposed else 1), rows, width), jnp.float32),
            *gives,
        ],
        scratch_shapes=[
            pltpu.VMEM((clusters * (1 if transposed else 3), rows, double), jnp.bfloat16),
            pltpu.VMEM((first.shape[0], rows, 2 * rank), jnp.bfloat16),
            *[pltpu.SMEM(t.shape, t.dtype) for t in tables],
            pltpu.SemaphoreType.DMA((len(tables),)),
        ],
        compiler_params=pltpu.CompilerParams(vmem_limit_bytes=VMEM_BYTES),
        cost_estimate=pl.CostEstimate(flops=flops, bytes_accessed=20_000_000, transcendentals=0),
    )(*tables, *fields, first, second, near)


def load_kernel(parts, *refs):
    count = (len(refs) - 1) // 2
    sources, targets, sems = refs[:count], refs[count : 2 * count], refs[2 * count]
    copies = []
    for i, (source, target) in enumerate(zip(sources, targets)):
        length = source.shape[0] // parts
        for k in range(parts):
            at = pl.ds(k * length, length)
            copies.append(pltpu.make_async_copy(source.at[at], target.at[at], sems.at[i, k]))
    for copy in copies:
        copy.start()
    for copy in copies:
        copy.wait()


def loaded(*arrays):
    return pl.pallas_call(
        functools.partial(load_kernel, LOADS),
        in_specs=[pl.BlockSpec(memory_space=pltpu.HBM)] * len(arrays),
        out_specs=[pl.BlockSpec(memory_space=pltpu.VMEM)] * len(arrays),
        out_shape=[jax.ShapeDtypeStruct(a.shape, a.dtype) for a in arrays],
        scratch_shapes=[pltpu.SemaphoreType.DMA((len(arrays), LOADS))],
        compiler_params=pltpu.CompilerParams(vmem_limit_bytes=LOAD_BYTES),
        cost_estimate=pl.CostEstimate(flops=0, bytes_accessed=12_000_000, transcendentals=0),
    )(*arrays)


def table_kernel(params, weights, counts, spread, places):
    slots, panels = params.shape
    high, width = spread.shape[0], places.shape[0]
    shift = width.bit_length() - 1
    high_ids = lax.broadcasted_iota(jnp.int32, (high, width), 0)
    low_ids = lax.broadcasted_iota(jnp.int32, (width, width), 0)
    slot_ids = lax.broadcasted_iota(jnp.int32, (slots, width), 0)
    for c in range(panels // width):
        at = slice(c * width, (c + 1) * width)
        value = jnp.where(slot_ids < counts[:, at], weights[:, at], 0.0)
        ids = params[:, at]
        high_of, low_of = ids >> shift, ids & (width - 1)
        for m in range(slots):
            row = slice(m, m + 1)
            to = slice((c * slots + m) * width, (c * slots + m + 1) * width)
            spread[:, to] = jnp.where(high_ids == high_of[row], value[row], 0.0)
            places[:, to] = jnp.where(low_ids == low_of[row], 1.0, 0.0).astype(jnp.bfloat16)


def gradient_tables(params, weights, counts, high, width):
    vmem = pl.BlockSpec(memory_space=pltpu.VMEM)
    entries = params.size
    return pl.pallas_call(
        table_kernel,
        in_specs=[vmem] * 3,
        out_specs=[vmem] * 2,
        out_shape=[
            jax.ShapeDtypeStruct((high, entries), jnp.float32),
            jax.ShapeDtypeStruct((width, entries), jnp.bfloat16),
        ],
        compiler_params=pltpu.CompilerParams(vmem_limit_bytes=VMEM_BYTES),
        cost_estimate=pl.CostEstimate(flops=0, bytes_accessed=8_000_000, transcendentals=0),
    )(params, weights, counts)


def final_kernel(column_total, n_fwd, n_adj, *refs):
    fwd_terms = refs[:n_fwd]
    adj_terms = refs[n_fwd : n_fwd + n_adj]
    spread, places, fwd_out, adj_out, grad, scaled = refs[n_fwd + n_adj :]
    clusters, height, _ = fwd_out.shape
    high, width = grad.shape
    entries = spread.shape[1] // clusters
    slots = entries // width
    for c in range(clusters):
        fwd = sum(t[c, : 2 * height].astype(jnp.float32) for t in fwd_terms)
        adj = sum(t[c, : 2 * height].astype(jnp.float32) for t in adj_terms)
        for out, value in ((fwd_out, fwd), (adj_out, adj)):
            out[c, :, :width] = value[:height]
            out[c, :, width:] = value[height:]
        product = fwd * adj
        sens = jnp.sum(product[:height] - product[height:], axis=0, keepdims=True) / column_total
        at = slice(c * entries, (c + 1) * entries)
        value = spread[:, at] * jnp.concatenate([sens] * slots, axis=1)
        top = value.astype(jnp.bfloat16)
        scaled[:high, at] = top
        scaled[high:, at] = (value - top.astype(jnp.float32)).astype(jnp.bfloat16)
    got = lax.dot_general(
        scaled[...], places[...], (((1,), (1,)), ((), ())), preferred_element_type=jnp.float32
    )
    grad[...] = got[:high] + got[high:]


def finish(column_total, shape, fwd_terms, adj_terms, spread, places):
    high, width = spread.shape[0], places.shape[0]
    vmem = pl.BlockSpec(memory_space=pltpu.VMEM)
    terms = [*fwd_terms, *adj_terms]
    field = jax.ShapeDtypeStruct(shape, jnp.float32)
    return pl.pallas_call(
        functools.partial(final_kernel, column_total, len(fwd_terms), len(adj_terms)),
        in_specs=[vmem] * (len(terms) + 2),
        out_specs=[vmem] * 3,
        out_shape=[field, field, jax.ShapeDtypeStruct((high, width), jnp.float32)],
        scratch_shapes=[pltpu.VMEM((2 * high, spread.shape[1]), jnp.bfloat16)],
        compiler_params=pltpu.CompilerParams(vmem_limit_bytes=VMEM_BYTES),
        cost_estimate=pl.CostEstimate(flops=200_000_000, bytes_accessed=3_000_000, transcendentals=0),
    )(*terms, spread, places)


def shards(
    forward_rhs,
    adjoint_rhs,
    far_clusters,
    far_ranks,
    far_left,
    far_right,
    near_clusters,
    near_blocks,
    panel_params,
    panel_weights,
    panel_counts,
):
    groups = lax.axis_size("clus")
    members = lax.axis_size("sub")
    clusters = forward_rhs.shape[0]
    total = clusters * groups
    column_total = forward_rhs.shape[1] * members
    evens = range(0, members, 2)

    height = forward_rhs.shape[1]
    part, rows = 2 * height, 2 * height * members
    tie = lax.optimization_barrier

    w_mine = [adjoint_rhs if m == 0 else moved(adjoint_rhs, 0, m) for m in evens]
    x_chip = [forward_rhs, moved(forward_rhs, 0, 1)]
    x_ring = jnp.concatenate([round_ring(x) for x in x_chip], axis=0)
    x_own = [forward_rhs if m == 0 else moved(forward_rhs, 0, m) for m in evens]
    left, right, near = loaded(far_left, far_right, near_blocks)
    x_ring, x_own, left, right, near = tie((x_ring, x_own, left, right, near))
    w_pieces = [x for m in range(0, members, 2) for x in (w_mine[m // 2], moved(w_mine[m // 2], 0, 1))]
    x_pieces = [*x_chip]
    for x in x_own[1:]:
        x_pieces += [x, moved(x, 0, 1)]
    x_side = [x_ring if m == 0 else moved(x_ring, 0, m) for m in evens]

    w_pieces, x_pieces = tie((w_pieces, x_pieces))
    apply = functools.partial(
        apply_blocks, total=total, members=members, far_ids=far_clusters, ranks=far_ranks, near_ids=near_clusters
    )
    adj, *give = apply(True, fields=w_pieces, first=left, second=right, near=near)
    x_side, _ = tie((x_side, adj))
    x_here = jnp.concatenate(x_side, axis=0)
    x_there = moved(x_here, 0, 1)

    def rows_of(field, m):
        return field[:, m * part : (m + 2) * part]

    given = [moved(x, 0, 1) for x in give]

    def chip_sums(m):
        return rows_of(adj[clusters : 2 * clusters], m) + given[m // 2].astype(jnp.float32)

    sides = [moved(chip_sums(m).astype(jnp.bfloat16), 0, m) for m in evens if m]
    odd_rows = [adj[:clusters, m * part : (m + 1) * part] for m in range(1, members, 2)]
    x_there, odd_rows = tie((x_there, odd_rows))
    adj_core = moved(jnp.concatenate(odd_rows, axis=1), 0, 1)
    fwd, = apply(False, fields=[*x_pieces, x_here, x_there], first=right, second=left, near=near)
    fwd, sides, adj_core, given[0] = tie((fwd, sides, adj_core, given[0]))

    def own_sum(field, core_part, m):
        k = m // 2
        return field[:clusters, m * part : (m + 1) * part] + core_part[:, k * part : (k + 1) * part]

    fwd_core = moved(
        jnp.concatenate([fwd[:, m * part : (m + 1) * part] for m in range(1, members, 2)], axis=1), 0, 1
    )
    side = chip_sums(0)
    for s in sides:
        side = side + s.astype(jnp.float32)
    side = side.astype(jnp.bfloat16)
    panel_params, side = tie((panel_params, side))
    spread, places = gradient_tables(
        panel_params, panel_weights, panel_counts[None, :],
        PAR_DEV * groups * members // near_blocks.shape[-1], near_blocks.shape[-1],
    )
    ring = round_ring(side)
    own = [moved(own_sum(adj, adj_core, m).astype(jnp.bfloat16), 0, m) for m in evens[1:]]
    over = [moved(own_sum(fwd, fwd_core, m).astype(jnp.bfloat16), 0, m) for m in evens[1:]]
    ring, over = tie((ring, over))
    ring_core = moved(ring[:, part:], 0, 1)
    forward_field, adjoint_field, grad = finish(
        column_total, forward_rhs.shape, [fwd, fwd_core, *over], [adj, adj_core, *own, ring, ring_core], spread, places
    )
    devices = groups * members
    pieces = lax.all_to_all(grad.reshape(devices, PAR_DEV), AXES, 0, 0, tiled=True)
    return forward_field, adjoint_field, jnp.sum(pieces, axis=0)


def solution(mesh):
    in_specs = (
        P("clus", "sub", None),
        P("clus", "sub", None),
        P(None, ("clus", "sub")),
        P(("clus", "sub")),
        P(("clus", "sub"), None, None, None),
        P(("clus", "sub"), None, None, None),
        P(None, ("clus", "sub")),
        P(("clus", "sub"), None, None, None),
        P(None, "clus"),
        P(None, "clus"),
        P("clus"),
    )
    out_specs = (P("clus", "sub", None), P("clus", "sub", None), P(("clus", "sub")))
    return jax.shard_map(shards, mesh=mesh, in_specs=in_specs, out_specs=out_specs, check_vma=False)
```

```python
import functools

import jax
import jax.numpy as jnp
from jax import lax
from jax.experimental import pallas as pl
from jax.experimental.pallas import tpu as pltpu
from jax.sharding import PartitionSpec as P

PAR_DEV = 128
AXES = ("clus", "sub")
LOADS = 4
VMEM_BYTES = 40 * 1024 * 1024
LOAD_BYTES = 46 * 1024 * 1024


def moved(x, by, mask):
    groups, members = lax.axis_size("clus"), lax.axis_size("sub")
    pairs = [
        (g * members + s, ((g + by) % groups) * members + (s ^ mask))
        for g in range(groups)
        for s in range(members)
    ]
    return lax.ppermute(x, AXES, pairs)


def round_ring(x, mask=0):
    groups, members = lax.axis_size("clus"), lax.axis_size("sub")
    pairs = [
        (g * members + s, ((g + 1 - 2 * (s % 2)) % groups) * members + (s ^ mask))
        for g in range(groups)
        for s in range(members)
    ]
    return lax.ppermute(x, AXES, pairs)


def wide_place(cluster, row, clusters, total, previous_first):
    first = row - lax.rem(row, clusters)
    place = lax.rem(cluster - first + total, total)
    near = lax.rem(place, clusters)
    following = jnp.where(previous_first, 2 * clusters, clusters)
    preceding = 3 * clusters - following
    side = jnp.where(place < 2 * clusters, following, preceding)
    return jnp.where(place < clusters, place, side + near)


def block_kernel(transposed, total, members, *refs):
    tables_in = refs[:3]
    count = members if transposed else members + 2
    fields = refs[3 : 3 + count]
    first, second, near, out, *give = refs[3 + count : -6]
    lhs, coeffs, far_ids, ranks, near_ids, sems = refs[-6:]
    tables = (far_ids, ranks, near_ids)
    copies = [pltpu.make_async_copy(a, b, sems.at[i]) for i, (a, b) in enumerate(zip(tables_in, tables))]
    for copy in copies:
        copy.start()

    height = fields[0].shape[1]
    clusters = fields[0].shape[0]
    far, _, rank, width = first.shape
    near_total = near.shape[0]
    rows = lhs.shape[1]
    core = lax.rem(lax.axis_index("sub"), 2)
    previous_first = core == (1 if transposed else 0)
    out[...] = jnp.zeros_like(out)

    def build(place, pieces):
        left, right = [], []
        for piece in pieces:
            x = piece.astype(jnp.float32)
            re, im = x[:, :width], x[:, width:]
            left += [re, im]
            right += [-im, re]
        both = [jnp.concatenate(left, axis=0), jnp.concatenate(right, axis=0)]
        lhs[place] = jnp.concatenate(both, axis=1).astype(jnp.bfloat16)

    @pl.loop(0, clusters, unroll=4)
    def _(c):
        build(c, [field[c] for field in fields[:members]])

    if not transposed:

        @pl.loop(0, clusters, unroll=4)
        def _(c):
            here, there = fields[members:]
            build(clusters + c, [here[m * clusters + c] for m in range(members)])
            build(2 * clusters + c, [there[(m ^ 1) * clusters + c] for m in range(members)])

    for copy in copies:
        copy.wait()

    def places(ids, b):
        row = ids[0, b]
        column = wide_place(ids[1, b], row, clusters, total, previous_first)
        row = lax.rem(row, clusters)
        return (row, column) if transposed else (column, row)

    rank_ids = lax.broadcasted_iota(jnp.int32, (rows, 2 * rank), 1)
    rank_ids = jnp.where(rank_ids >= rank, rank_ids - rank, rank_ids)

    for b in range(far):
        re, im = first[b, 0], first[b, 1]
        factor = jnp.concatenate(
            [jnp.concatenate([re, im], axis=1), jnp.concatenate([-im, re], axis=1)], axis=0
        )
        coeff = lax.dot_general(
            lhs[places(far_ids, b)[0]],
            factor,
            (((1,), (1,)), ((), ())),
            preferred_element_type=jnp.float32,
        )
        coeffs[b] = jnp.where(rank_ids < ranks[b], coeff, 0.0).astype(jnp.bfloat16)
    for b in range(far):
        out[places(far_ids, b)[1]] += jnp.dot(
            coeffs[b], second[b].reshape(2 * rank, width), preferred_element_type=jnp.float32
        )
    for b in range(near_total):
        source, place = places(near_ids, b)
        if transposed:
            value = jnp.dot(
                lhs[source], near[b].reshape(2 * width, width), preferred_element_type=jnp.float32
            )
        else:
            value = lax.dot_general(
                lhs[source],
                jnp.concatenate([near[b, 0], near[b, 1]], axis=1),
                (((1,), (1,)), ((), ())),
                preferred_element_type=jnp.float32,
            )
        out[place] += value
    part = 2 * height
    for k, half in enumerate(give):
        rows_here = out[2 * clusters :, 2 * k * part : (2 * k + 2) * part]
        half[...] = jnp.concatenate([rows_here[:, part:], rows_here[:, :part]], axis=1).astype(half.dtype)


def apply_blocks(transposed, total, members, far_ids, ranks, near_ids, fields, first, second, near):
    clusters, height, double = fields[0].shape
    rows = members * 2 * height
    rank, width = first.shape[2:]
    anywhere = pl.BlockSpec(memory_space=pl.ANY)
    vmem = pl.BlockSpec(memory_space=pltpu.VMEM)
    tables = (far_ids, ranks, near_ids)
    give = jax.ShapeDtypeStruct((clusters, 4 * height, width), jnp.bfloat16)
    gives = [give] * (members // 2) if transposed else []
    flops = 2 * rows * (first.shape[0] * 2 * 2 * rank * 2 * width + near.shape[0] * 2 * width * width)
    return pl.pallas_call(
        functools.partial(block_kernel, transposed, total, members),
        in_specs=[anywhere] * 3 + [vmem] * (len(fields) + 3),
        out_specs=[vmem] * (1 + len(gives)),
        out_shape=[
            jax.ShapeDtypeStruct((clusters * (3 if transposed else 1), rows, width), jnp.float32),
            *gives,
        ],
        scratch_shapes=[
            pltpu.VMEM((clusters * (1 if transposed else 3), rows, double), jnp.bfloat16),
            pltpu.VMEM((first.shape[0], rows, 2 * rank), jnp.bfloat16),
            *[pltpu.SMEM(t.shape, t.dtype) for t in tables],
            pltpu.SemaphoreType.DMA((len(tables),)),
        ],
        compiler_params=pltpu.CompilerParams(vmem_limit_bytes=VMEM_BYTES),
        cost_estimate=pl.CostEstimate(flops=flops, bytes_accessed=20_000_000, transcendentals=0),
    )(*tables, *fields, first, second, near)


def load_kernel(parts, *refs):
    count = (len(refs) - 1) // 2
    sources, targets, sems = refs[:count], refs[count : 2 * count], refs[2 * count]
    copies = []
    for i, (source, target) in enumerate(zip(sources, targets)):
        length = source.shape[0] // parts
        for k in range(parts):
            at = pl.ds(k * length, length)
            copies.append(pltpu.make_async_copy(source.at[at], target.at[at], sems.at[i, k]))
    for copy in copies:
        copy.start()
    for copy in copies:
        copy.wait()


def loaded(*arrays):
    return pl.pallas_call(
        functools.partial(load_kernel, LOADS),
        in_specs=[pl.BlockSpec(memory_space=pltpu.HBM)] * len(arrays),
        out_specs=[pl.BlockSpec(memory_space=pltpu.VMEM)] * len(arrays),
        out_shape=[jax.ShapeDtypeStruct(a.shape, a.dtype) for a in arrays],
        scratch_shapes=[pltpu.SemaphoreType.DMA((len(arrays), LOADS))],
        compiler_params=pltpu.CompilerParams(vmem_limit_bytes=LOAD_BYTES),
        cost_estimate=pl.CostEstimate(flops=0, bytes_accessed=12_000_000, transcendentals=0),
    )(*arrays)


def table_kernel(params, weights, counts, spread, places):
    slots, panels = params.shape
    high, width = spread.shape[0], places.shape[0]
    shift = width.bit_length() - 1
    high_ids = lax.broadcasted_iota(jnp.int32, (high, width), 0)
    low_ids = lax.broadcasted_iota(jnp.int32, (width, width), 0)
    slot_ids = lax.broadcasted_iota(jnp.int32, (slots, width), 0)
    for c in range(panels // width):
        at = slice(c * width, (c + 1) * width)
        value = jnp.where(slot_ids < counts[:, at], weights[:, at], 0.0)
        ids = params[:, at]
        high_of, low_of = ids >> shift, ids & (width - 1)
        for m in range(slots):
            row = slice(m, m + 1)
            to = slice((c * slots + m) * width, (c * slots + m + 1) * width)
            spread[:, to] = jnp.where(high_ids == high_of[row], value[row], 0.0)
            places[:, to] = jnp.where(low_ids == low_of[row], 1.0, 0.0).astype(jnp.bfloat16)


def gradient_tables(params, weights, counts, high, width):
    vmem = pl.BlockSpec(memory_space=pltpu.VMEM)
    entries = params.size
    return pl.pallas_call(
        table_kernel,
        in_specs=[vmem] * 3,
        out_specs=[vmem] * 2,
        out_shape=[
            jax.ShapeDtypeStruct((high, entries), jnp.float32),
            jax.ShapeDtypeStruct((width, entries), jnp.bfloat16),
        ],
        compiler_params=pltpu.CompilerParams(vmem_limit_bytes=VMEM_BYTES),
        cost_estimate=pl.CostEstimate(flops=0, bytes_accessed=8_000_000, transcendentals=0),
    )(params, weights, counts)


def final_kernel(column_total, n_fwd, n_adj, *refs):
    fwd_terms = refs[:n_fwd]
    adj_terms = refs[n_fwd : n_fwd + n_adj]
    spread, places, fwd_out, adj_out, grad, scaled, fwd_held, adj_held, sems = refs[n_fwd + n_adj :]
    clusters, height, _ = fwd_out.shape
    high, width = grad.shape
    entries = spread.shape[1] // clusters
    slots = entries // width
    chunk = clusters // LOADS
    copies = []
    for c in range(clusters):
        fwd = sum(t[c, : 2 * height].astype(jnp.float32) for t in fwd_terms)
        adj = sum(t[c, : 2 * height].astype(jnp.float32) for t in adj_terms)
        for held, value in ((fwd_held, fwd), (adj_held, adj)):
            held[c, :, :width] = value[:height]
            held[c, :, width:] = value[height:]
        product = fwd * adj
        sens = jnp.sum(product[:height] - product[height:], axis=0, keepdims=True) / column_total
        at = slice(c * entries, (c + 1) * entries)
        value = spread[:, at] * jnp.concatenate([sens] * slots, axis=1)
        top = value.astype(jnp.bfloat16)
        scaled[:high, at] = top
        scaled[high:, at] = (value - top.astype(jnp.float32)).astype(jnp.bfloat16)
        if (c + 1) % chunk == 0:
            k = c // chunk
            part = pl.ds(k * chunk, chunk)
            for i, (held, out) in enumerate(((fwd_held, fwd_out), (adj_held, adj_out))):
                copies.append(pltpu.make_async_copy(held.at[part], out.at[part], sems.at[i, k]))
                copies[-1].start()
    got = lax.dot_general(
        places[...], scaled[...], (((1,), (1,)), ((), ())), preferred_element_type=jnp.float32
    )
    grad[...] = jnp.transpose(got[:, :high] + got[:, high:])
    for copy in copies:
        copy.wait()


def finish(column_total, shape, fwd_terms, adj_terms, spread, places):
    high, width = spread.shape[0], places.shape[0]
    vmem = pl.BlockSpec(memory_space=pltpu.VMEM)
    terms = [*fwd_terms, *adj_terms]
    field = jax.ShapeDtypeStruct(shape, jnp.float32)
    return pl.pallas_call(
        functools.partial(final_kernel, column_total, len(fwd_terms), len(adj_terms)),
        in_specs=[vmem] * (len(terms) + 2),
        out_specs=[pl.BlockSpec(memory_space=pl.ANY)] * 2 + [vmem],
        out_shape=[field, field, jax.ShapeDtypeStruct((high, width), jnp.float32)],
        scratch_shapes=[
            pltpu.VMEM((2 * high, spread.shape[1]), jnp.bfloat16),
            pltpu.VMEM(shape, jnp.float32),
            pltpu.VMEM(shape, jnp.float32),
            pltpu.SemaphoreType.DMA((2, LOADS)),
        ],
        compiler_params=pltpu.CompilerParams(vmem_limit_bytes=VMEM_BYTES),
        cost_estimate=pl.CostEstimate(flops=200_000_000, bytes_accessed=3_000_000, transcendentals=0),
    )(*terms, spread, places)


def shards(
    forward_rhs,
    adjoint_rhs,
    far_clusters,
    far_ranks,
    far_left,
    far_right,
    near_clusters,
    near_blocks,
    panel_params,
    panel_weights,
    panel_counts,
):
    groups = lax.axis_size("clus")
    members = lax.axis_size("sub")
    clusters = forward_rhs.shape[0]
    total = clusters * groups
    column_total = forward_rhs.shape[1] * members
    evens = range(0, members, 2)

    height = forward_rhs.shape[1]
    part, rows = 2 * height, 2 * height * members
    tie = lax.optimization_barrier

    w_mine = [adjoint_rhs if m == 0 else moved(adjoint_rhs, 0, m) for m in evens]
    x_chip = [forward_rhs, moved(forward_rhs, 0, 1)]
    x_ring = jnp.concatenate([round_ring(x) for x in x_chip], axis=0)
    x_own = [forward_rhs if m == 0 else moved(forward_rhs, 0, m) for m in evens]
    left, right, near = loaded(far_left, far_right, near_blocks)
    x_ring, x_own, left, right, near = tie((x_ring, x_own, left, right, near))
    w_pieces = [x for m in range(0, members, 2) for x in (w_mine[m // 2], moved(w_mine[m // 2], 0, 1))]
    x_pieces = [*x_chip]
    for x in x_own[1:]:
        x_pieces += [x, moved(x, 0, 1)]
    x_side = [x_ring if m == 0 else moved(x_ring, 0, m) for m in evens]

    w_pieces, x_pieces = tie((w_pieces, x_pieces))
    apply = functools.partial(
        apply_blocks, total=total, members=members, far_ids=far_clusters, ranks=far_ranks, near_ids=near_clusters
    )
    adj, *give = apply(True, fields=w_pieces, first=left, second=right, near=near)
    x_side, _ = tie((x_side, adj))
    x_here = jnp.concatenate(x_side, axis=0)
    x_there = moved(x_here, 0, 1)

    def rows_of(field, m):
        return field[:, m * part : (m + 2) * part]

    given = [moved(x, 0, 1) for x in give]

    def chip_sums(m):
        return rows_of(adj[clusters : 2 * clusters], m) + given[m // 2].astype(jnp.float32)

    sides = [moved(chip_sums(m).astype(jnp.bfloat16), 0, m) for m in evens if m]
    odd_rows = [adj[:clusters, m * part : (m + 1) * part] for m in range(1, members, 2)]
    x_there, odd_rows = tie((x_there, odd_rows))
    adj_core = moved(jnp.concatenate(odd_rows, axis=1), 0, 1)
    fwd, = apply(False, fields=[*x_pieces, x_here, x_there], first=right, second=left, near=near)
    fwd, sides, adj_core, given[0] = tie((fwd, sides, adj_core, given[0]))

    def own_sum(field, core_part, m):
        k = m // 2
        return field[:clusters, m * part : (m + 1) * part] + core_part[:, k * part : (k + 1) * part]

    fwd_core = moved(
        jnp.concatenate([fwd[:, m * part : (m + 1) * part] for m in range(1, members, 2)], axis=1), 0, 1
    )
    side = chip_sums(0)
    for s in sides:
        side = side + s.astype(jnp.float32)
    side = side.astype(jnp.bfloat16)
    panel_params, side = tie((panel_params, side))
    spread, places = gradient_tables(
        panel_params, panel_weights, panel_counts[None, :],
        PAR_DEV * groups * members // near_blocks.shape[-1], near_blocks.shape[-1],
    )
    ring = [round_ring(side[:, k * part : (k + 1) * part], k) for k in range(2)]
    own = [moved(own_sum(adj, adj_core, m).astype(jnp.bfloat16), 0, m) for m in evens[1:]]
    over = [moved(own_sum(fwd, fwd_core, m).astype(jnp.bfloat16), 0, m) for m in evens[1:]]
    forward_field, adjoint_field, grad = finish(
        column_total, forward_rhs.shape, [fwd, fwd_core, *over], [adj, adj_core, *own, *ring], spread, places
    )
    devices = groups * members
    pieces = lax.all_to_all(grad.reshape(devices, PAR_DEV), AXES, 0, 0, tiled=True)
    return forward_field, adjoint_field, jnp.sum(pieces, axis=0)


def solution(mesh):
    in_specs = (
        P("clus", "sub", None),
        P("clus", "sub", None),
        P(None, ("clus", "sub")),
        P(("clus", "sub")),
        P(("clus", "sub"), None, None, None),
        P(("clus", "sub"), None, None, None),
        P(None, ("clus", "sub")),
        P(("clus", "sub"), None, None, None),
        P(None, "clus"),
        P(None, "clus"),
        P("clus"),
    )
    out_specs = (P("clus", "sub", None), P("clus", "sub", None), P(("clus", "sub")))
    return jax.shard_map(shards, mesh=mesh, in_specs=in_specs, out_specs=out_specs, check_vma=False)
```

```python
import functools

import jax
import jax.numpy as jnp
from jax import lax
from jax.experimental import pallas as pl
from jax.experimental.pallas import tpu as pltpu
from jax.sharding import PartitionSpec as P

PAR_DEV = 128
AXES = ("clus", "sub")
LOADS = 4
VMEM_BYTES = 40 * 1024 * 1024
LOAD_BYTES = 46 * 1024 * 1024


def moved(x, by, mask):
    groups, members = lax.axis_size("clus"), lax.axis_size("sub")
    pairs = [
        (g * members + s, ((g + by) % groups) * members + (s ^ mask))
        for g in range(groups)
        for s in range(members)
    ]
    return lax.ppermute(x, AXES, pairs)


def round_ring(x, mask=0):
    groups, members = lax.axis_size("clus"), lax.axis_size("sub")
    pairs = [
        (g * members + s, ((g + 1 - 2 * (s % 2)) % groups) * members + (s ^ mask))
        for g in range(groups)
        for s in range(members)
    ]
    return lax.ppermute(x, AXES, pairs)


def wide_place(cluster, row, clusters, total, previous_first):
    first = row - lax.rem(row, clusters)
    place = lax.rem(cluster - first + total, total)
    near = lax.rem(place, clusters)
    following = jnp.where(previous_first, 2 * clusters, clusters)
    preceding = 3 * clusters - following
    side = jnp.where(place < 2 * clusters, following, preceding)
    return jnp.where(place < clusters, place, side + near)


def block_kernel(transposed, total, members, *refs):
    tables_in = refs[:3]
    count = members if transposed else members + 2
    fields = refs[3 : 3 + count]
    first, second, near, out, *give = refs[3 + count : -6]
    lhs, coeffs, far_ids, ranks, near_ids, sems = refs[-6:]
    tables = (far_ids, ranks, near_ids)
    copies = [pltpu.make_async_copy(a, b, sems.at[i]) for i, (a, b) in enumerate(zip(tables_in, tables))]
    for copy in copies:
        copy.start()

    height = fields[0].shape[1]
    clusters = fields[0].shape[0]
    far, _, rank, width = first.shape
    near_total = near.shape[0]
    rows = lhs.shape[1]
    core = lax.rem(lax.axis_index("sub"), 2)
    previous_first = core == (1 if transposed else 0)
    out[...] = jnp.zeros_like(out)

    def build(place, pieces):
        left, right = [], []
        for piece in pieces:
            x = piece.astype(jnp.float32)
            re, im = x[:, :width], x[:, width:]
            left += [re, im]
            right += [-im, re]
        both = [jnp.concatenate(left, axis=0), jnp.concatenate(right, axis=0)]
        lhs[place] = jnp.concatenate(both, axis=1).astype(jnp.bfloat16)

    @pl.loop(0, clusters, unroll=4)
    def _(c):
        build(c, [field[c] for field in fields[:members]])

    if not transposed:

        @pl.loop(0, clusters, unroll=4)
        def _(c):
            here, there = fields[members:]
            build(clusters + c, [here[m * clusters + c] for m in range(members)])
            build(2 * clusters + c, [there[(m ^ 1) * clusters + c] for m in range(members)])

    for copy in copies:
        copy.wait()

    def places(ids, b):
        row = ids[0, b]
        column = wide_place(ids[1, b], row, clusters, total, previous_first)
        row = lax.rem(row, clusters)
        return (row, column) if transposed else (column, row)

    rank_ids = lax.broadcasted_iota(jnp.int32, (rows, 2 * rank), 1)
    rank_ids = jnp.where(rank_ids >= rank, rank_ids - rank, rank_ids)

    for b in range(far):
        re, im = first[b, 0], first[b, 1]
        factor = jnp.concatenate(
            [jnp.concatenate([re, im], axis=1), jnp.concatenate([-im, re], axis=1)], axis=0
        )
        coeff = lax.dot_general(
            lhs[places(far_ids, b)[0]],
            factor,
            (((1,), (1,)), ((), ())),
            preferred_element_type=jnp.float32,
        )
        coeffs[b] = jnp.where(rank_ids < ranks[b], coeff, 0.0).astype(jnp.bfloat16)
    for b in range(far):
        out[places(far_ids, b)[1]] += jnp.dot(
            coeffs[b], second[b].reshape(2 * rank, width), preferred_element_type=jnp.float32
        )
    for b in range(near_total):
        source, place = places(near_ids, b)
        if transposed:
            value = jnp.dot(
                lhs[source], near[b].reshape(2 * width, width), preferred_element_type=jnp.float32
            )
        else:
            value = lax.dot_general(
                lhs[source],
                jnp.concatenate([near[b, 0], near[b, 1]], axis=1),
                (((1,), (1,)), ((), ())),
                preferred_element_type=jnp.float32,
            )
        out[place] += value
    part = 2 * height
    for k, half in enumerate(give):
        rows_here = out[2 * clusters :, 2 * k * part : (2 * k + 2) * part]
        half[...] = jnp.concatenate([rows_here[:, part:], rows_here[:, :part]], axis=1).astype(half.dtype)


def apply_blocks(transposed, total, members, far_ids, ranks, near_ids, fields, first, second, near):
    clusters, height, double = fields[0].shape
    rows = members * 2 * height
    rank, width = first.shape[2:]
    anywhere = pl.BlockSpec(memory_space=pl.ANY)
    vmem = pl.BlockSpec(memory_space=pltpu.VMEM)
    tables = (far_ids, ranks, near_ids)
    give = jax.ShapeDtypeStruct((clusters, 4 * height, width), jnp.bfloat16)
    gives = [give] * (members // 2) if transposed else []
    flops = 2 * rows * (first.shape[0] * 2 * 2 * rank * 2 * width + near.shape[0] * 2 * width * width)
    return pl.pallas_call(
        functools.partial(block_kernel, transposed, total, members),
        in_specs=[anywhere] * 3 + [vmem] * (len(fields) + 3),
        out_specs=[vmem] * (1 + len(gives)),
        out_shape=[
            jax.ShapeDtypeStruct((clusters * (3 if transposed else 1), rows, width), jnp.float32),
            *gives,
        ],
        scratch_shapes=[
            pltpu.VMEM((clusters * (1 if transposed else 3), rows, double), jnp.bfloat16),
            pltpu.VMEM((first.shape[0], rows, 2 * rank), jnp.bfloat16),
            *[pltpu.SMEM(t.shape, t.dtype) for t in tables],
            pltpu.SemaphoreType.DMA((len(tables),)),
        ],
        compiler_params=pltpu.CompilerParams(vmem_limit_bytes=VMEM_BYTES),
        cost_estimate=pl.CostEstimate(flops=flops, bytes_accessed=20_000_000, transcendentals=0),
    )(*tables, *fields, first, second, near)


def load_kernel(parts, *refs):
    count = (len(refs) - 1) // 2
    sources, targets, sems = refs[:count], refs[count : 2 * count], refs[2 * count]
    copies = []
    for i, (source, target) in enumerate(zip(sources, targets)):
        length = source.shape[0] // parts
        for k in range(parts):
            at = pl.ds(k * length, length)
            copies.append(pltpu.make_async_copy(source.at[at], target.at[at], sems.at[i, k]))
    for copy in copies:
        copy.start()
    for copy in copies:
        copy.wait()


def loaded(*arrays):
    return pl.pallas_call(
        functools.partial(load_kernel, LOADS),
        in_specs=[pl.BlockSpec(memory_space=pltpu.HBM)] * len(arrays),
        out_specs=[pl.BlockSpec(memory_space=pltpu.VMEM)] * len(arrays),
        out_shape=[jax.ShapeDtypeStruct(a.shape, a.dtype) for a in arrays],
        scratch_shapes=[pltpu.SemaphoreType.DMA((len(arrays), LOADS))],
        compiler_params=pltpu.CompilerParams(vmem_limit_bytes=LOAD_BYTES),
        cost_estimate=pl.CostEstimate(flops=0, bytes_accessed=12_000_000, transcendentals=0),
    )(*arrays)


def table_kernel(params, weights, counts, spread, places):
    slots, panels = params.shape
    high, width = spread.shape[0], places.shape[0]
    shift = width.bit_length() - 1
    high_ids = lax.broadcasted_iota(jnp.int32, (high, width), 0)
    low_ids = lax.broadcasted_iota(jnp.int32, (width, width), 0)
    slot_ids = lax.broadcasted_iota(jnp.int32, (slots, width), 0)
    for c in range(panels // width):
        at = slice(c * width, (c + 1) * width)
        value = jnp.where(slot_ids < counts[:, at], weights[:, at], 0.0)
        ids = params[:, at]
        high_of, low_of = ids >> shift, ids & (width - 1)
        for m in range(slots):
            row = slice(m, m + 1)
            to = slice((c * slots + m) * width, (c * slots + m + 1) * width)
            spread[:, to] = jnp.where(high_ids == high_of[row], value[row], 0.0)
            places[:, to] = jnp.where(low_ids == low_of[row], 1.0, 0.0).astype(jnp.bfloat16)


def gradient_tables(params, weights, counts, high, width):
    vmem = pl.BlockSpec(memory_space=pltpu.VMEM)
    entries = params.size
    return pl.pallas_call(
        table_kernel,
        in_specs=[vmem] * 3,
        out_specs=[vmem] * 2,
        out_shape=[
            jax.ShapeDtypeStruct((high, entries), jnp.float32),
            jax.ShapeDtypeStruct((width, entries), jnp.bfloat16),
        ],
        compiler_params=pltpu.CompilerParams(vmem_limit_bytes=VMEM_BYTES),
        cost_estimate=pl.CostEstimate(flops=0, bytes_accessed=8_000_000, transcendentals=0),
    )(params, weights, counts)


def final_kernel(column_total, n_fwd, n_adj, *refs):
    fwd_terms = refs[:n_fwd]
    adj_terms = refs[n_fwd : n_fwd + n_adj]
    spread, places, fwd_out, adj_out, grad, scaled, fwd_held, adj_held, sems = refs[n_fwd + n_adj :]
    clusters, height, _ = fwd_out.shape
    high, width = grad.shape
    entries = spread.shape[1] // clusters
    slots = entries // width
    chunk = clusters // LOADS
    copies = []
    for c in range(clusters):
        fwd = sum(t[c, : 2 * height].astype(jnp.float32) for t in fwd_terms)
        adj = sum(t[c, : 2 * height].astype(jnp.float32) for t in adj_terms)
        for held, value in ((fwd_held, fwd), (adj_held, adj)):
            held[c, :, :width] = value[:height]
            held[c, :, width:] = value[height:]
        product = fwd * adj
        sens = jnp.sum(product[:height] - product[height:], axis=0, keepdims=True) / column_total
        at = slice(c * entries, (c + 1) * entries)
        value = spread[:, at] * jnp.concatenate([sens] * slots, axis=1)
        top = value.astype(jnp.bfloat16)
        scaled[:high, at] = top
        scaled[high:, at] = (value - top.astype(jnp.float32)).astype(jnp.bfloat16)
        if (c + 1) % chunk == 0:
            k = c // chunk
            part = pl.ds(k * chunk, chunk)
            for i, (held, out) in enumerate(((fwd_held, fwd_out), (adj_held, adj_out))):
                copies.append(pltpu.make_async_copy(held.at[part], out.at[part], sems.at[i, k]))
                copies[-1].start()
    got = lax.dot_general(
        places[...], scaled[...], (((1,), (1,)), ((), ())), preferred_element_type=jnp.float32
    )
    grad[...] = jnp.transpose(got[:, :high] + got[:, high:])
    for copy in copies:
        copy.wait()


def finish(column_total, shape, fwd_terms, adj_terms, spread, places):
    high, width = spread.shape[0], places.shape[0]
    vmem = pl.BlockSpec(memory_space=pltpu.VMEM)
    terms = [*fwd_terms, *adj_terms]
    field = jax.ShapeDtypeStruct(shape, jnp.float32)
    return pl.pallas_call(
        functools.partial(final_kernel, column_total, len(fwd_terms), len(adj_terms)),
        in_specs=[vmem] * (len(terms) + 2),
        out_specs=[pl.BlockSpec(memory_space=pl.ANY)] * 2 + [vmem],
        out_shape=[field, field, jax.ShapeDtypeStruct((high, width), jnp.float32)],
        scratch_shapes=[
            pltpu.VMEM((2 * high, spread.shape[1]), jnp.bfloat16),
            pltpu.VMEM(shape, jnp.float32),
            pltpu.VMEM(shape, jnp.float32),
            pltpu.SemaphoreType.DMA((2, LOADS)),
        ],
        compiler_params=pltpu.CompilerParams(vmem_limit_bytes=VMEM_BYTES),
        cost_estimate=pl.CostEstimate(flops=200_000_000, bytes_accessed=3_000_000, transcendentals=0),
    )(*terms, spread, places)


def shards(
    forward_rhs,
    adjoint_rhs,
    far_clusters,
    far_ranks,
    far_left,
    far_right,
    near_clusters,
    near_blocks,
    panel_params,
    panel_weights,
    panel_counts,
):
    groups = lax.axis_size("clus")
    members = lax.axis_size("sub")
    clusters = forward_rhs.shape[0]
    total = clusters * groups
    column_total = forward_rhs.shape[1] * members
    evens = range(0, members, 2)

    height = forward_rhs.shape[1]
    part, rows = 2 * height, 2 * height * members
    tie = lax.optimization_barrier

    w_mine = [adjoint_rhs if m == 0 else moved(adjoint_rhs, 0, m) for m in evens]
    x_chip = [forward_rhs, moved(forward_rhs, 0, 1)]
    x_ring = jnp.concatenate([round_ring(x) for x in x_chip], axis=0)
    x_own = [forward_rhs if m == 0 else moved(forward_rhs, 0, m) for m in evens]
    left, right, near = loaded(far_left, far_right, near_blocks)
    x_ring, x_own, left, right, near = tie((x_ring, x_own, left, right, near))
    w_pieces = [x for m in range(0, members, 2) for x in (w_mine[m // 2], moved(w_mine[m // 2], 0, 1))]
    x_pieces = [*x_chip]
    for x in x_own[1:]:
        x_pieces += [x, moved(x, 0, 1)]
    x_side = [x_ring if m == 0 else moved(x_ring, 0, m) for m in evens]

    w_pieces, x_pieces = tie((w_pieces, x_pieces))
    apply = functools.partial(
        apply_blocks, total=total, members=members, far_ids=far_clusters, ranks=far_ranks, near_ids=near_clusters
    )
    adj, *give = apply(True, fields=w_pieces, first=left, second=right, near=near)
    x_side, _ = tie((x_side, adj))
    x_here = jnp.concatenate(x_side, axis=0)
    x_there = moved(x_here, 0, 1)

    def rows_of(field, m):
        return field[:, m * part : (m + 2) * part]

    given = [moved(x, 0, 1) for x in give]

    def chip_sums(m):
        return rows_of(adj[clusters : 2 * clusters], m) + given[m // 2].astype(jnp.float32)

    sides = [moved(chip_sums(m).astype(jnp.bfloat16), 0, m) for m in evens if m]
    odd_rows = [adj[:clusters, m * part : (m + 1) * part] for m in range(1, members, 2)]
    x_there, odd_rows = tie((x_there, odd_rows))
    adj_core = moved(jnp.concatenate(odd_rows, axis=1), 0, 1)
    fwd, = apply(False, fields=[*x_pieces, x_here, x_there], first=right, second=left, near=near)
    fwd_core = moved(
        jnp.concatenate([fwd[:, m * part : (m + 1) * part] for m in range(1, members, 2)], axis=1), 0, 1
    )
    fwd, sides, adj_core, given[0] = tie((fwd, sides, adj_core, given[0]))

    def own_sum(field, core_part, m):
        k = m // 2
        return field[:clusters, m * part : (m + 1) * part] + core_part[:, k * part : (k + 1) * part]

    side = chip_sums(0)
    for s in sides:
        side = side + s.astype(jnp.float32)
    side = side.astype(jnp.bfloat16)
    panel_params, side = tie((panel_params, side))
    spread, places = gradient_tables(
        panel_params, panel_weights, panel_counts[None, :],
        PAR_DEV * groups * members // near_blocks.shape[-1], near_blocks.shape[-1],
    )
    ring = [round_ring(side[:, k * part : (k + 1) * part], k) for k in range(2)]
    own = [moved(own_sum(adj, adj_core, m).astype(jnp.bfloat16), 0, m) for m in evens[1:]]
    over = [moved(own_sum(fwd, fwd_core, m).astype(jnp.bfloat16), 0, m) for m in evens[1:]]
    forward_field, adjoint_field, grad = finish(
        column_total, forward_rhs.shape, [fwd, fwd_core, *over], [adj, adj_core, *own, *ring], spread, places
    )
    devices = groups * members
    pieces = lax.all_to_all(grad.reshape(devices, PAR_DEV), AXES, 0, 0, tiled=True)
    return forward_field, adjoint_field, jnp.sum(pieces, axis=0)


def solution(mesh):
    in_specs = (
        P("clus", "sub", None),
        P("clus", "sub", None),
        P(None, ("clus", "sub")),
        P(("clus", "sub")),
        P(("clus", "sub"), None, None, None),
        P(("clus", "sub"), None, None, None),
        P(None, ("clus", "sub")),
        P(("clus", "sub"), None, None, None),
        P(None, "clus"),
        P(None, "clus"),
        P("clus"),
    )
    out_specs = (P("clus", "sub", None), P("clus", "sub", None), P(("clus", "sub")))
    return jax.shard_map(shards, mesh=mesh, in_specs=in_specs, out_specs=out_specs, check_vma=False)
```
